256 devices in a mesh: dom: 64 (over z, y, core), rep: 4 (over x).
Axes of the slice: x: 4, y: 4, z: 8, core: 2. Of those that a mesh axis runs over, the one named last changes fastest.
Arguments:
- node_input: bfloat16 [1048576, 256], P(('dom', 'rep')), may hold values from -6 to 6
- neighbor_first: int32 [262144, 15], P(('dom', 'rep')), may hold values from 0 to 4095
- neighbor_second: int32 [32768, 10], P(('dom', 'rep')), may hold values from 0 to 1023
- merge_ids: int32 [256, 4096], P(('dom', 'rep')), may hold values from 0 to 2047, never falling along the last dimension, each value on 1 to 4 neighbouring positions
- owner_ids: int32 [524288, 1], P(('dom', 'rep')), may hold values from 0 to 63; in each aligned block of 2048 rows (0 to 2047, 2048 to 4095, ...) at most 40 rows name the same one
- owner_rows: int32 [524288], P(('dom', 'rep')), may hold values from 0 to 2047
- cotangent: bfloat16 [32768, 256], P(('dom', 'rep')), may hold values from -6 to 6
- self_first: bfloat16 [256, 256], replicated, may hold values from -0.375 to 0.375
- agg_first: bfloat16 [256, 256], replicated, may hold values from -0.375 to 0.375
- self_second: bfloat16 [256, 256], replicated, may hold values from -0.375 to 0.375
- agg_second: bfloat16 [256, 256], replicated, may hold values from -0.375 to 0.375
Outputs:
- emb_grad: float32 [131072, 256], P('dom')
- weight_grads: float32 [4, 256, 256], replicated
The draws below stay inside these ranges and needn't reach their ends.
Inputs may be any that keep to these rules, and one draw needn't show every extreme that they name: `owner_ids`: among one device's 2048 distinct nodes no partition is named more than 40 times, a bound that some block reaches. `merge_ids`: along one device's row the ids never fall; each of the 2048 ids covers 1 to 4 consecutive rows.
All inputs are finite; a program needn't handle non-finite values.
Results may differ from the reference program's by a relative error of at most 0.0042.
Values sent between devices are 32-bit elements; how exact they have to be, the bound alone decides.
No kernel may reach another device: no remote copies, remote signals or barrier semaphores. Data moves between devices by JAX's collectives and lax.ppermute only.
A program may use at most 128 MiB of HBM per device.

```python
import math
import jax
import jax.numpy as jnp
import numpy as np
from jax import lax

D = 256
F1 = 15
F2 = 10
BATCH = 128
N1 = 1024
N0 = 4096
UNIQ = 2048
ROWS_OWN = 2048
CAP = 40
N_DOM = 64
DEVICES = 256


def set_ends(array, stream_key, low, top_value):
    extent = array.shape
    place = [jax.random.randint(jax.random.fold_in(stream_key, axis), (), 0, extent[axis]) for axis in range(len(extent))]
    array = array.at[tuple(place)].set(low)
    longest = extent.index(max(extent))
    place[longest] = (place[longest] + 1) % extent[longest]
    return array.at[tuple(place)].set(top_value)


def block_scale(own_key, extent, shards, low, high):
    level, own = 1.0, jax.random.fold_in(own_key, 6)
    for axis_at, shards_of in shards:
        steps = jnp.exp(jax.random.uniform(jax.random.fold_in(own, axis_at), (shards_of,), jnp.float32, low / len(shards), high / len(shards)))
        level = level * jnp.repeat(steps, extent[axis_at] // shards_of).reshape([-1 if axis == axis_at else 1 for axis in range(len(extent))])
    return level


def profile(amount, total, reach, slope):
    weights = [(1 << 20) // math.isqrt(grade ** slope) + 1 for grade in range(2, amount + 1)]
    spare, holding = total - reach - (amount - 1), [1] * (amount - 1)
    while spare > 0:
        candidates = [i for i in range(amount - 1) if holding[i] < reach]
        mass, remaining = sum([weights[i] for i in candidates]), spare
        for i in candidates:
            more = min(reach - holding[i], max(1, remaining * weights[i] // mass), spare)
            holding[i] = holding[i] + more
            spare = spare - more
    return np.array([reach] + holding)


def uneven_parts(own_key, amount, total, limit, slope):
    if amount == 2:
        one = jax.random.randint(own_key, (), max(1, total - limit), min(limit, total - 1) + 1)
        return jnp.stack([one, total - one])
    sizes = jnp.asarray(profile(amount, total, limit, slope), jnp.int32)
    twos = (amount - 1) // 2
    source_of, sink = sizes[1:1 + 2 * twos:2], sizes[2:2 + 2 * twos:2]
    room = jnp.minimum(source_of - 1, limit - sink)
    passed = jax.random.randint(jax.random.fold_in(own_key, 1), (twos,), 0, 1 << 20) % (room + 1)
    sizes = sizes.at[1:1 + 2 * twos:2].set(source_of - passed).at[2:2 + 2 * twos:2].set(sink + passed)
    return sizes[jax.random.permutation(jax.random.fold_in(own_key, 2), amount)]


def shared_out(key, own, number, rows, count, top, bound, slope):
    order = jax.random.permutation(key, count)
    packed, common = load_shares(count, rows * top, bound, slope, True), load_shares(count, rows * top, bound, slope, False)
    places = jnp.arange(count)

    def named(tallies, turn):
        used = int((tallies > 0).sum())
        fixed = max(1, used // 4)
        passed = fixed + (places - fixed + turn * (used - fixed)) % max(1, count - fixed)
        return jnp.zeros((count,), jnp.int32).at[order[jnp.where(places < fixed, places, passed)]].set(jnp.asarray(tallies, jnp.int32))

    tallies = jnp.where(number % 4 == 0, named(packed, number // 4), named(common, number - number // 4 - 1))
    mixed = jax.random.permutation(jax.random.fold_in(own, 3), count)
    source_of, taker = mixed[0:count // 2 * 2:2], mixed[1:count // 2 * 2:2]
    slack = jnp.minimum(tallies[source_of] - 1, bound - tallies[taker]) // 2
    slack = jnp.where((source_of == order[0]) | (taker == order[0]) | (tallies[taker] == 0), 0, jnp.maximum(slack, 0))
    passed = jax.random.randint(jax.random.fold_in(own, 4), (count // 2,), 0, 1 << 20) % (slack + 1)
    tallies = tallies.at[source_of].add(-passed).at[taker].add(passed)
    members = jnp.searchsorted(jnp.cumsum(tallies), jnp.arange(rows * top), side="right").astype(jnp.int32)
    listing = members.reshape(top, rows).T
    listing = listing[jax.random.permutation(jax.random.fold_in(own, 1), rows)]
    turn = jax.random.randint(jax.random.fold_in(own, 2), (rows, 1), 0, top)
    return jnp.take_along_axis(listing, (jnp.arange(top)[None, :] + turn) % top, axis=1)


def load_shares(number_of, total, reach, skew, full):
    weights = [(1 << 20) // math.isqrt(standing ** skew) + 1 for standing in range(1, number_of + 1)]
    largest = reach if full else min(reach, max(-(-total // number_of), total * weights[0] // sum(weights)))
    least = 1 if total - largest >= number_of - 1 else 0
    counts, surplus = [largest] + [least] * (number_of - 1), total - largest - least * (number_of - 1)
    while surplus > 0:
        free = [i for i in range(1, number_of) if counts[i] < largest] or [i for i in range(1, number_of) if counts[i] < reach]
        mass, remaining = sum([weights[i] for i in free]), surplus
        for i in free:
            extra = min(reach - counts[i], max(1, remaining * weights[i] // mass), surplus)
            counts[i] = counts[i] + extra
            surplus = surplus - extra
    return np.array(counts)


def bell_draw(stream_key, dims, deviation, bound, pieces=(), dtype=jnp.bfloat16):
    values = jax.random.normal(stream_key, dims, jnp.float32) * deviation
    if len(pieces) > 0:
        values = block_scale(stream_key, dims, pieces, -0.22, 0.18) * values
    return jnp.clip(values, min=-bound, max=bound).astype(dtype)


def setup_inputs(seed: int = 0) -> dict:
    key_of = jax.random.split(jax.random.key(seed), 12)
    node_input = bell_draw(key_of[0], (N0 * DEVICES, D), 1.0, 6.0, ((0, 256),))
    neighbor_first = set_ends(jax.random.randint(key_of[1], (N1 * DEVICES, F1), 0, N0), jax.random.fold_in(key_of[1], 1), 0, N0 - 1).astype(jnp.int32)
    neighbor_second = set_ends(jax.random.randint(key_of[2], (BATCH * DEVICES, F2), 0, N1), jax.random.fold_in(key_of[2], 1), 0, N1 - 1).astype(jnp.int32)
    merge_ids = jax.vmap(lambda own: jnp.searchsorted(jnp.cumsum(uneven_parts(own, UNIQ, N0, 4, 1)), jnp.arange(N0), side="right"))(jax.random.split(key_of[3], DEVICES)).reshape((DEVICES, N0)).astype(jnp.int32)
    owner_ids_keys = jax.random.split(jax.random.fold_in(key_of[4], 1), (UNIQ * DEVICES) // UNIQ)
    owner_ids_turns = jax.random.permutation(jax.random.fold_in(key_of[4], 3), (UNIQ * DEVICES) // UNIQ)
    owner_ids = jax.vmap(lambda own, number: shared_out(jax.random.fold_in(key_of[4], 2), own, number, UNIQ, N_DOM, 1, CAP, 2))(owner_ids_keys, owner_ids_turns).reshape((UNIQ * DEVICES, 1))
    owner_rows = set_ends(jax.random.randint(key_of[5], (UNIQ * DEVICES,), 0, ROWS_OWN), jax.random.fold_in(key_of[5], 1), 0, ROWS_OWN - 1).astype(jnp.int32)
    cotangent = bell_draw(key_of[6], (BATCH * DEVICES, D), 1.0, 6.0, ((0, 256),))
    self_first = bell_draw(key_of[7], (D, D), D ** -0.5, 0.375)
    agg_first = bell_draw(key_of[8], (D, D), D ** -0.5, 0.375)
    self_second = bell_draw(key_of[9], (D, D), D ** -0.5, 0.375)
    agg_second = bell_draw(key_of[10], (D, D), D ** -0.5, 0.375)
    return dict(node_input=node_input, neighbor_first=neighbor_first, neighbor_second=neighbor_second, merge_ids=merge_ids, owner_ids=owner_ids, owner_rows=owner_rows, cotangent=cotangent, self_first=self_first, agg_first=agg_first, self_second=self_second, agg_second=agg_second)


grad_scale = 16.0


def silu_slope(preact):
    sigmoid = jax.nn.sigmoid(preact)
    return sigmoid * (1.0 + preact * (1.0 - sigmoid))


def device_pass(node_input, neighbor_first, neighbor_second, merge_ids, cotangent, self_first, agg_first, self_second, agg_second):
    widened = node_input.astype(jnp.float32)
    mean_one = (jnp.sum(widened[neighbor_first], axis=1) / F1).astype(jnp.bfloat16)
    preact = jnp.dot(node_input[:N1], self_first, preferred_element_type=jnp.float32) + jnp.dot(mean_one, agg_first, preferred_element_type=jnp.float32)
    hidden = jax.nn.silu(preact).astype(jnp.bfloat16)
    mean_two = (jnp.sum(hidden.astype(jnp.float32)[neighbor_second], axis=1) / F2).astype(jnp.bfloat16)
    g_self2 = jnp.dot(hidden[:BATCH].T, cotangent, preferred_element_type=jnp.float32)
    g_agg2 = jnp.dot(mean_two.T, cotangent, preferred_element_type=jnp.float32)
    down_two = (jnp.dot(cotangent, agg_second.T, preferred_element_type=jnp.float32) / F2).astype(jnp.bfloat16)
    hidden_grad = jnp.zeros((N1, D), jnp.float32).at[neighbor_second.reshape(-1)].add(jnp.repeat(down_two.astype(jnp.float32), F2, axis=0))
    hidden_grad = hidden_grad.at[:BATCH].add(jnp.dot(cotangent, self_second.T, preferred_element_type=jnp.float32))
    pre_grad = (hidden_grad * silu_slope(preact)).astype(jnp.bfloat16)
    g_self1 = jnp.dot(node_input[:N1].T, pre_grad, preferred_element_type=jnp.float32)
    g_agg1 = jnp.dot(mean_one.T, pre_grad, preferred_element_type=jnp.float32)
    down_one = (jnp.dot(pre_grad, agg_first.T, preferred_element_type=jnp.float32) / F1).astype(jnp.bfloat16)
    input_grad = jnp.zeros((N0, D), jnp.float32).at[neighbor_first.reshape(-1)].add(jnp.repeat(down_one.astype(jnp.float32), F1, axis=0))
    input_grad = input_grad.at[:N1].add(jnp.dot(pre_grad, self_first.T, preferred_element_type=jnp.float32))
    input_grad = input_grad.astype(jnp.bfloat16)
    merged = jax.ops.segment_sum(input_grad.astype(jnp.float32), merge_ids, num_segments=UNIQ) * grad_scale
    return jnp.stack([g_self1, g_agg1, g_self2, g_agg2]), merged


def reference(node_input, neighbor_first, neighbor_second, merge_ids, owner_ids, owner_rows, cotangent, self_first, agg_first, self_second, agg_second):
    inputs_all = node_input.reshape(DEVICES, N0, D)
    first_all = neighbor_first.reshape(DEVICES, N1, F1)
    second_all = neighbor_second.reshape(DEVICES, BATCH, F2)
    owners_all = owner_ids.reshape(DEVICES, UNIQ)
    rows_all = owner_rows.reshape(DEVICES, UNIQ)
    cot_all = cotangent.reshape(DEVICES, BATCH, D)

    def step_device(carry, slices):
        table, weights = carry
        inputs, first, second, ids, owners, rows, cot = slices
        grads, merged = device_pass(inputs, first, second, ids, cot, self_first, agg_first, self_second, agg_second)
        places = (owners * ROWS_OWN + rows).astype(jnp.int32)
        return (table.at[places].add(merged), weights + grads), None

    start_table = jnp.zeros((N_DOM * ROWS_OWN, D), jnp.float32)
    start_weights = jnp.zeros((4, D, D), jnp.float32)
    (table, weights), _ = lax.scan(step_device, (start_table, start_weights), (inputs_all, first_all, second_all, merge_ids, owners_all, rows_all, cot_all))
    return table, weights * (DEVICES * BATCH) ** -0.5
```

```python
import functools

import jax
import jax.numpy as jnp
from jax import lax
from jax.experimental import pallas as pl
from jax.experimental.pallas import tpu as pltpu
from jax.sharding import PartitionSpec as P

ROWS_OWN = 2048
GRAD_SCALE = 16.0
NIBBLES = 8
NIBBLE_BITS = 4
SPAN = 256
LANES = 128
REPS = 4
F32 = jnp.float32
BF16 = jnp.bfloat16
NN = (((1,), (0,)), ((), ()))
NT = (((1,), (1,)), ((), ()))


def matmul(a, b, dims=NN):
    return lax.dot_general(a, b, dims, preferred_element_type=F32)


def sigmoid(v):
    return 1.0 / (1.0 + jnp.exp(-v))


def local_kernel(
    capacity,
    x_ref,
    first_ref,
    second_ref,
    ids_ref,
    ids_smem,
    owners_ref,
    rows_ref,
    cot_ref,
    self1_ref,
    agg1_ref,
    self2_ref,
    agg2_ref,
    out_ref,
    grads_ref,
    xt_ref,
    table_ref,
    mean_ref,
    down_ref,
    selfgrad_ref,
    spread_ref,
    merged_ref,
    picked_ref,
    target_ref,
    high_ref,
    low_ref,
):
    inputs, width = x_ref.shape
    fan1, firsts = first_ref.shape
    fan2, batch = second_ref.shape
    uniq = owners_ref.shape[1]
    domains = high_ref.shape[0]
    words = inputs // NIBBLES
    lanes = 128
    depth = 64

    eye = (
        lax.broadcasted_iota(jnp.int32, (width, width), 0)
        == lax.broadcasted_iota(jnp.int32, (width, width), 1)
    ).astype(BF16)

    def turn(c, _):
        at = pl.multiple_of(c * 512, 512)
        xt_ref[:, pl.ds(at, 512)] = matmul(eye, x_ref[pl.ds(at, 512), :], NT).astype(BF16)
        return 0

    lax.fori_loop(0, inputs // 512, turn, 0)

    def count(step, _):
        col = pl.multiple_of((step // (words // depth)) * lanes, lanes)
        row = pl.multiple_of((step % (words // depth)) * depth, depth)
        nodes = first_ref[:, pl.ds(col, lanes)]
        keys = nodes % words
        values = jnp.left_shift(jnp.int32(1), (nodes // words) * NIBBLE_BITS)
        place = lax.broadcasted_iota(jnp.int32, (depth, lanes), 0) + row
        total = jnp.zeros((depth, lanes), jnp.int32)
        for k in range(fan1):
            total = total + jnp.where(keys[k : k + 1, :] == place, values[k : k + 1, :], 0)
        for part in range(NIBBLES):
            counts = jnp.bitwise_and(jnp.right_shift(total, part * NIBBLE_BITS), 15)
            table_ref[pl.ds(part * words + row, depth), pl.ds(col, lanes)] = counts.astype(
                F32
            ).astype(BF16)
        return 0

    lax.fori_loop(0, (firsts // lanes) * (words // depth), count, 0)

    def mean(c, _):
        at = pl.multiple_of(c * SPAN, SPAN)
        mean_ref[:, pl.ds(at, SPAN)] = (
            matmul(xt_ref[...], table_ref[:, pl.ds(at, SPAN)]) / fan1
        ).astype(BF16)
        return 0

    lax.fori_loop(0, firsts // SPAN, mean, 0)

    mean_one = mean_ref[...]
    selfs = xt_ref[:, :firsts]
    contract_first = (((0,), (0,)), ((), ()))
    preact = matmul(self1_ref[...], selfs, contract_first) + matmul(
        agg1_ref[...], mean_one, contract_first
    )
    gate = sigmoid(preact)
    hidden = (preact * gate).astype(BF16)
    second = jnp.zeros((firsts, batch), F32)
    place2 = lax.broadcasted_iota(jnp.int32, (firsts, batch), 0)
    for k in range(fan2):
        second = second + (second_ref[k : k + 1, :] == place2).astype(F32)
    second = second.astype(BF16)
    mean_two = (matmul(hidden, second) / fan2).astype(BF16)
    cot = cot_ref[...]
    grads_ref[2 * width : 3 * width, :] = matmul(hidden[:, :batch], cot)
    grads_ref[3 * width :, :] = matmul(mean_two, cot)
    down_two = (matmul(agg2_ref[...], cot, NT) / fan2).astype(BF16)
    hidden_grad = matmul(down_two, second, NT)
    targets_grad = hidden_grad[:, :batch] + matmul(self2_ref[...], cot, NT)
    hidden_grad = jnp.concatenate([targets_grad, hidden_grad[:, batch:]], axis=1)
    pre_grad = (hidden_grad * (gate * (1.0 + preact * (1.0 - gate)))).astype(BF16)
    grads_ref[:width, :] = matmul(selfs, pre_grad, NT)
    grads_ref[width : 2 * width, :] = matmul(mean_one, pre_grad, NT)
    down_ref[...] = (matmul(agg1_ref[...], pre_grad) / fan1).astype(BF16)
    selfgrad_ref[...] = matmul(self1_ref[...], pre_grad)

    step_rows = 512
    for c in range(firsts // step_rows):
        at = c * step_rows
        spread_ref[:, at : at + step_rows] = (
            matmul(down_ref[...], table_ref[at : at + step_rows, :], NT)
            + selfgrad_ref[:, at : at + step_rows]
        ).astype(BF16)

    def spread(c, _):
        at = pl.multiple_of(c * step_rows, step_rows)
        spread_ref[:, pl.ds(at, step_rows)] = matmul(
            down_ref[...], table_ref[pl.ds(at, step_rows), :], NT
        ).astype(BF16)
        return 0

    lax.fori_loop(firsts // step_rows, inputs // step_rows, spread, 0)

    window = SPAN + 8
    merged_ref[...] = jnp.zeros(merged_ref.shape, F32)

    def merge(c, _):
        at = pl.multiple_of(c * SPAN, SPAN)
        low = jnp.minimum(ids_smem[0, at] // 8, (uniq - window) // 8) * 8
        low = pl.multiple_of(low, 8)
        place = lax.broadcasted_iota(jnp.int32, (window, SPAN), 0) + low
        picker = (ids_ref[:, pl.ds(at, SPAN)] == place).astype(F32).astype(BF16)
        merged_ref[pl.ds(low, window), :] += matmul(picker, spread_ref[:, pl.ds(at, SPAN)], NT)
        return 0

    lax.fori_loop(0, inputs // SPAN, merge, 0)
    picked_ref[...] = (merged_ref[...] * GRAD_SCALE).astype(BF16)

    upper = (
        lax.broadcasted_iota(jnp.int32, (SPAN, SPAN), 0)
        < lax.broadcasted_iota(jnp.int32, (SPAN, SPAN), 1)
    ).astype(BF16)
    domain = lax.broadcasted_iota(jnp.int32, (domains, SPAN), 0)
    half = capacity // 2
    tall = half + 1
    slot_place = lax.broadcasted_iota(jnp.int32, (LANES, SPAN), 0)
    carry = jnp.zeros((domains, 1), F32)
    high = jnp.zeros((domains, LANES), F32)
    low = jnp.zeros((domains, LANES), F32)
    for c in range(uniq // SPAN):
        at = c * SPAN
        owners = owners_ref[:, at : at + SPAN]
        marks = (owners == domain).astype(F32)
        marks_b = marks.astype(BF16)
        earlier = matmul(marks_b, upper) + carry
        slots = jnp.sum(earlier * marks, axis=0, keepdims=True).astype(jnp.int32)
        carry = carry + jnp.sum(marks, axis=1, keepdims=True)
        base = owners * tall + slots
        target_ref[0:1, at : at + SPAN] = jnp.where(slots < half, base, -1)
        target_ref[1:2, at : at + SPAN] = jnp.where(slots < half, -1, base - half)
        codes = rows_ref[:, at : at + SPAN] + 1
        here = slots == slot_place
        high = high + matmul(marks_b, jnp.where(here, codes // 16, 0).astype(F32).astype(BF16), NT)
        low = low + matmul(marks_b, jnp.where(here, codes % 16, 0).astype(F32).astype(BF16), NT)
    high_ref[...] = high
    low_ref[...] = low

    group = 8
    chunk = group * tall
    quarter = width // REPS
    label_line = (
        lax.broadcasted_iota(jnp.int32, (chunk, group), 0)
        == lax.broadcasted_iota(jnp.int32, (chunk, group), 1) * tall + half
    ).astype(F32).astype(BF16)

    def place_rows(c, _):
        at = pl.multiple_of(c * chunk, chunk)
        doms = pl.ds(pl.multiple_of(c * group, group), group)
        place = lax.broadcasted_iota(jnp.int32, (chunk, uniq), 0) + at
        first_half = matmul(
            (target_ref[0:1, :] == place).astype(F32).astype(BF16), picked_ref[...]
        )
        second_half = matmul(
            (target_ref[1:2, :] == place).astype(F32).astype(BF16), picked_ref[...]
        )
        labels = matmul(label_line, high_ref[doms, :].astype(BF16)) * 16.0 + matmul(
            label_line, low_ref[doms, :].astype(BF16)
        )
        for r in range(REPS):
            columns = slice(r * quarter, (r + 1) * quarter)
            line = jnp.concatenate([first_half[:, columns], second_half[:, columns]], axis=1)
            out_ref[pl.ds(pl.multiple_of(r * domains * tall + at, 8), chunk), :] = line + labels
        return 0

    lax.fori_loop(0, domains // group, place_rows, 0)


def add_kernel(capacity, lines_ref, table_ref):
    half = capacity // 2
    tall = half + 1
    group = 32
    chunk = group * tall
    sources = lines_ref.shape[0] // tall
    quarter = LANES // 2
    height = table_ref.shape[0]

    def spot(shape, axis):
        index = lax.broadcasted_iota(jnp.int32, shape, axis)
        source = index // tall
        return source, index - source * tall

    def one(mask):
        return mask.astype(F32).astype(BF16)

    line_source, line_slot = spot((LANES, chunk), 1)
    lane = lax.broadcasted_iota(jnp.int32, (LANES, chunk), 0)
    real = line_slot < half
    spread_first = one((lane == line_slot) & real)
    spread_second = one((lane == line_slot + half) & real)
    mine = line_source[:group, :] == lax.broadcasted_iota(jnp.int32, (group, chunk), 0)
    col_source, _ = spot((chunk, group), 0)
    expand = one(col_source == lax.broadcasted_iota(jnp.int32, (chunk, group), 1))
    _, col_slot = spot((chunk, LANES), 0)
    col_lane = lax.broadcasted_iota(jnp.int32, (chunk, LANES), 1)
    col_real = col_slot < half
    at_first = (col_lane == col_slot) & col_real
    at_second = (col_lane == col_slot + half) & col_real
    left = col_lane < quarter
    place = lax.broadcasted_iota(jnp.int32, (height, chunk), 0)
    table_ref[...] = jnp.zeros(table_ref.shape, F32)

    def step(c, _):
        at = pl.multiple_of(c * chunk, 8)
        codes = lines_ref[pl.ds(at + half, group, stride=tall), :]
        lines = lines_ref[pl.ds(at, chunk), :]
        swapped = pltpu.roll(lines, quarter, 1)
        high = jnp.floor(codes * (1.0 / 16.0))
        low = (codes - high * 16.0).astype(BF16)
        high = high.astype(BF16)
        grown = matmul(expand, high) * 16.0 + matmul(expand, low)
        total = jnp.zeros(table_ref.shape, F32)
        for spread, at_column, pair in (
            (spread_first, at_first, jnp.where(left, lines, swapped)),
            (spread_second, at_second, jnp.where(left, swapped, lines)),
        ):
            flat = matmul(high, spread) * 16.0 + matmul(low, spread)
            row = jnp.sum(jnp.where(mine, flat, 0.0), axis=0, keepdims=True).astype(jnp.int32) - 1
            column = jnp.sum(jnp.where(at_column, grown, 0.0), axis=1, keepdims=True)
            column = column.astype(jnp.int32) - 1
            block = jnp.where(column < 0, -1, jnp.right_shift(column, 9))
            kept = [
                jnp.where(block == 2 * side + jnp.where(left, 0, 1), pair, 0.0).astype(BF16)
                for side in range(2)
            ]
            wide = jnp.concatenate(kept, axis=1)
            picker = one((row & (height - 1)) == place)
            total = total + matmul(picker, wide)
        table_ref[...] += total
        return 0

    lax.fori_loop(0, sources // group, step, 0)


def join_kernel(parts_ref, table_ref):
    height = parts_ref.shape[0] // REPS
    quarter = parts_ref.shape[1] // REPS
    for q in range(REPS):
        table_ref[q * height : (q + 1) * height, :] = jnp.concatenate(
            [
                parts_ref[r * height : (r + 1) * height, q * quarter : (q + 1) * quarter]
                for r in range(REPS)
            ],
            axis=1,
        )


VMEM = pl.BlockSpec(memory_space=pltpu.VMEM)
SMEM = pl.BlockSpec(memory_space=pltpu.SMEM)
PARAMS = pltpu.CompilerParams(vmem_limit_bytes=48 * 1024 * 1024)


def local_pass(capacity, domains, x, first, second, ids, owners, rows, cot, self1, agg1, self2, agg2):
    inputs, width = x.shape
    firsts = first.shape[1]
    uniq = owners.shape[1]
    return pl.pallas_call(
        functools.partial(local_kernel, capacity),
        out_shape=(
            jax.ShapeDtypeStruct((REPS * domains * (capacity // 2 + 1), LANES), F32),
            jax.ShapeDtypeStruct((4 * width, width), F32),
        ),
        in_specs=[VMEM] * 4 + [SMEM] + [VMEM] * 7,
        out_specs=(VMEM, VMEM),
        scratch_shapes=[
            pltpu.VMEM((width, inputs), BF16),
            pltpu.VMEM((inputs, firsts), BF16),
            pltpu.VMEM((width, firsts), BF16),
            pltpu.VMEM((width, firsts), BF16),
            pltpu.VMEM((width, firsts), F32),
            pltpu.VMEM((width, inputs), BF16),
            pltpu.VMEM((uniq, width), F32),
            pltpu.VMEM((uniq, width), BF16),
            pltpu.VMEM((2, uniq), jnp.int32),
            pltpu.VMEM((domains, LANES), F32),
            pltpu.VMEM((domains, LANES), F32),
        ],
        compiler_params=PARAMS,
        name="local_pass",
    )(x, first, second, ids, ids, owners, rows, cot, self1, agg1, self2, agg2)


def add_rows(capacity, lines):
    return pl.pallas_call(
        functools.partial(add_kernel, capacity),
        out_shape=jax.ShapeDtypeStruct((ROWS_OWN // REPS, 4 * (LANES // 2)), F32),
        in_specs=[VMEM],
        out_specs=VMEM,
        compiler_params=PARAMS,
        name="add_rows",
    )(lines)


def join_columns(parts):
    return pl.pallas_call(
        join_kernel,
        out_shape=jax.ShapeDtypeStruct(parts.shape, F32),
        in_specs=[VMEM],
        out_specs=VMEM,
        compiler_params=PARAMS,
        name="join_columns",
    )(parts)


def on_device(
    node_input,
    neighbor_first,
    neighbor_second,
    merge_ids,
    owner_ids,
    owner_rows,
    cotangent,
    self_first,
    agg_first,
    self_second,
    agg_second,
):
    target_total = cotangent.shape[0]
    width = node_input.shape[1]
    uniq_total = owner_rows.shape[0]
    domains = lax.axis_size("dom")
    factor = (domains * lax.axis_size("rep") * target_total) ** (-0.5)
    capacity = max(2, 5 * uniq_total // (4 * domains))
    outgoing, grads = local_pass(
        capacity,
        domains,
        node_input,
        neighbor_first.T,
        neighbor_second.T,
        merge_ids,
        owner_ids.T,
        owner_rows[None, :],
        cotangent,
        self_first,
        agg_first,
        self_second,
        agg_second,
    )
    arrived = lax.all_to_all(
        outgoing.reshape(REPS * domains, 1, -1), ("rep", "dom"), 0, 0, tiled=True
    )
    own_grads = lax.psum_scatter(grads, "rep", scatter_dimension=0, tiled=True)
    share = width // domains
    shares = lax.all_to_all(own_grads.reshape(domains, share, width), "dom", 0, 0, tiled=True)
    total = jnp.sum(shares, axis=0) * factor
    whole = lax.all_to_all(
        jnp.broadcast_to(total[None], (domains, share, width)), "dom", 0, 0, tiled=True
    ).reshape(width, width)
    weight_grads = lax.all_to_all(
        jnp.broadcast_to(whole[None], (REPS, width, width)), "rep", 0, 0, tiled=True
    )
    quarter = add_rows(capacity, arrived.reshape(-1, LANES))
    table = join_columns(lax.all_gather(quarter, "rep", axis=0, tiled=True))
    return (table, weight_grads)


def solution(mesh):
    placed = (
        P(("dom", "rep"), None),
        P(("dom", "rep"), None),
        P(("dom", "rep"), None),
        P(("dom", "rep"), None),
        P(("dom", "rep"), None),
        P(("dom", "rep")),
        P(("dom", "rep"), None),
        P(),
        P(),
        P(),
        P(),
    )
    return jax.shard_map(
        on_device, mesh=mesh, in_specs=placed, out_specs=(P("dom", None), P()), check_vma=False
    )
```

```python
import functools

import jax
import jax.numpy as jnp
from jax import lax
from jax.experimental import pallas as pl
from jax.experimental.pallas import tpu as pltpu
from jax.sharding import PartitionSpec as P

ROWS_OWN = 2048
GRAD_SCALE = 16.0
NIBBLES = 8
DEPTH = 256
GROUP = 32
NIBBLE_BITS = 4
SPAN = 256
LANES = 128
REPS = 4
F32 = jnp.float32
BF16 = jnp.bfloat16
NN = (((1,), (0,)), ((), ()))
NT = (((1,), (1,)), ((), ()))


def matmul(a, b, dims=NN):
    return lax.dot_general(a, b, dims, preferred_element_type=F32)


def sigmoid(v):
    return 1.0 / (1.0 + jnp.exp(-v))


def local_kernel(
    capacity,
    x_hbm,
    first_hbm,
    second_hbm,
    ids_hbm,
    owners_hbm,
    rows_hbm,
    cot_hbm,
    self1_hbm,
    agg1_hbm,
    self2_hbm,
    agg2_hbm,
    out_ref,
    grads_ref,
    xt_ref,
    table_ref,
    mean_ref,
    down_ref,
    selfgrad_ref,
    spread_ref,
    merged_ref,
    picked_ref,
    target_ref,
    high_ref,
    low_ref,
    x_ref,
    first_ref,
    second_ref,
    ids_ref,
    owners_ref,
    rows_ref,
    cot_ref,
    self1_ref,
    agg1_ref,
    self2_ref,
    agg2_ref,
    ids_smem,
    sems,
):
    sources = (
        (owners_hbm, owners_ref),
        (rows_hbm, rows_ref),
        (first_hbm, first_ref),
        (x_hbm, x_ref),
        (second_hbm, second_ref),
        (cot_hbm, cot_ref),
        (self1_hbm, self1_ref),
        (agg1_hbm, agg1_ref),
        (self2_hbm, self2_ref),
        (agg2_hbm, agg2_ref),
        (ids_hbm, ids_ref),
        (ids_hbm, ids_smem),
    )
    copies = [
        pltpu.make_async_copy(source, local, sems.at[n])
        for n, (source, local) in enumerate(sources)
    ]
    for copy in copies:
        copy.start()

    inputs, width = x_ref.shape
    fan1, firsts = first_ref.shape
    fan2, batch = second_ref.shape
    uniq = owners_ref.shape[1]
    domains = high_ref.shape[0]
    words = inputs // NIBBLES
    lanes = 128
    depth = DEPTH
    turned = inputs // ((firsts // lanes) * (words // depth))

    copies[0].wait()
    copies[1].wait()
    upper = (
        lax.broadcasted_iota(jnp.int32, (SPAN, SPAN), 0)
        < lax.broadcasted_iota(jnp.int32, (SPAN, SPAN), 1)
    ).astype(BF16)
    domain = lax.broadcasted_iota(jnp.int32, (domains, SPAN), 0)
    half = capacity // 2
    tall = half + 1
    slot_place = lax.broadcasted_iota(jnp.int32, (LANES, SPAN), 0)
    carry = jnp.zeros((domains, 1), F32)
    high = jnp.zeros((domains, LANES), F32)
    low = jnp.zeros((domains, LANES), F32)
    for c in range(uniq // SPAN):
        at = c * SPAN
        owners = owners_ref[:, at : at + SPAN]
        marks = (owners == domain).astype(F32)
        marks_b = marks.astype(BF16)
        earlier = matmul(marks_b, upper) + carry
        slots = jnp.sum(earlier * marks, axis=0, keepdims=True).astype(jnp.int32)
        carry = carry + jnp.sum(marks, axis=1, keepdims=True)
        base = owners * tall + slots
        target_ref[0:1, at : at + SPAN] = jnp.where(slots < half, base, -1)
        target_ref[1:2, at : at + SPAN] = jnp.where(slots < half, -1, base - half)
        codes = rows_ref[:, at : at + SPAN] + 1
        here = slots == slot_place
        high = high + matmul(marks_b, jnp.where(here, codes // 16, 0).astype(F32).astype(BF16), NT)
        low = low + matmul(marks_b, jnp.where(here, codes % 16, 0).astype(F32).astype(BF16), NT)
    high_ref[...] = high
    low_ref[...] = low

    eye = (
        lax.broadcasted_iota(jnp.int32, (width, width), 0)
        == lax.broadcasted_iota(jnp.int32, (width, width), 1)
    ).astype(BF16)

    copies[2].wait()
    copies[3].wait()

    def count(step, _):
        col = pl.multiple_of((step // (words // depth)) * lanes, lanes)
        row = pl.multiple_of((step % (words // depth)) * depth, depth)
        nodes = first_ref[:, pl.ds(col, lanes)]
        keys = nodes % words
        values = jnp.left_shift(jnp.int32(1), (nodes // words) * NIBBLE_BITS)
        place = lax.broadcasted_iota(jnp.int32, (depth, lanes), 0) + row
        total = jnp.zeros((depth, lanes), jnp.int32)
        for k in range(fan1):
            total = total + jnp.where(keys[k : k + 1, :] == place, values[k : k + 1, :], 0)
        for part in range(NIBBLES):
            counts = jnp.bitwise_and(jnp.right_shift(total, part * NIBBLE_BITS), 15)
            table_ref[pl.ds(part * words + row, depth), pl.ds(col, lanes)] = counts.astype(
                F32
            ).astype(BF16)
        at = pl.multiple_of(step * turned, turned)
        xt_ref[:, pl.ds(at, turned)] = matmul(eye, x_ref[pl.ds(at, turned), :], NT).astype(BF16)
        return 0

    lax.fori_loop(0, (firsts // lanes) * (words // depth), count, 0, unroll=2)

    def mean(c, _):
        at = pl.multiple_of(c * SPAN, SPAN)
        mean_ref[:, pl.ds(at, SPAN)] = (
            matmul(xt_ref[...], table_ref[:, pl.ds(at, SPAN)]) / fan1
        ).astype(BF16)
        return 0

    lax.fori_loop(0, firsts // SPAN, mean, 0, unroll=2)

    for copy in copies[4:]:
        copy.wait()
    mean_one = mean_ref[...]
    selfs = xt_ref[:, :firsts]
    contract_first = (((0,), (0,)), ((), ()))
    preact = matmul(self1_ref[...], selfs, contract_first) + matmul(
        agg1_ref[...], mean_one, contract_first
    )
    gate = sigmoid(preact)
    hidden = (preact * gate).astype(BF16)
    second = jnp.zeros((firsts, batch), F32)
    place2 = lax.broadcasted_iota(jnp.int32, (firsts, batch), 0)
    for k in range(fan2):
        second = second + (second_ref[k : k + 1, :] == place2).astype(F32)
    second = second.astype(BF16)
    mean_two = (matmul(hidden, second) / fan2).astype(BF16)
    cot = cot_ref[...]
    grads_ref[2 * width : 3 * width, :] = matmul(hidden[:, :batch], cot)
    grads_ref[3 * width :, :] = matmul(mean_two, cot)
    down_two = (matmul(agg2_ref[...], cot, NT) / fan2).astype(BF16)
    hidden_grad = matmul(down_two, second, NT)
    targets_grad = hidden_grad[:, :batch] + matmul(self2_ref[...], cot, NT)
    hidden_grad = jnp.concatenate([targets_grad, hidden_grad[:, batch:]], axis=1)
    pre_grad = (hidden_grad * (gate * (1.0 + preact * (1.0 - gate)))).astype(BF16)
    grads_ref[:width, :] = matmul(selfs, pre_grad, NT)
    grads_ref[width : 2 * width, :] = matmul(mean_one, pre_grad, NT)
    down_ref[...] = (matmul(agg1_ref[...], pre_grad) / fan1).astype(BF16)
    selfgrad_ref[...] = matmul(self1_ref[...], pre_grad)

    step_rows = 512
    for c in range(firsts // step_rows):
        at = c * step_rows
        spread_ref[:, at : at + step_rows] = (
            matmul(down_ref[...], table_ref[at : at + step_rows, :], NT)
            + selfgrad_ref[:, at : at + step_rows]
        ).astype(BF16)

    def spread(c, _):
        at = pl.multiple_of(c * step_rows, step_rows)
        spread_ref[:, pl.ds(at, step_rows)] = matmul(
            down_ref[...], table_ref[pl.ds(at, step_rows), :], NT
        ).astype(BF16)
        return 0

    lax.fori_loop(firsts // step_rows, inputs // step_rows, spread, 0, unroll=2)

    window = SPAN + 8
    merged_ref[...] = jnp.zeros(merged_ref.shape, F32)

    def merge(c, _):
        at = pl.multiple_of(c * SPAN, SPAN)
        low = jnp.minimum(ids_smem[0, at] // 8, (uniq - window) // 8) * 8
        low = pl.multiple_of(low, 8)
        place = lax.broadcasted_iota(jnp.int32, (window, SPAN), 0) + low
        picker = (ids_ref[:, pl.ds(at, SPAN)] == place).astype(F32).astype(BF16)
        merged_ref[pl.ds(low, window), :] += matmul(picker, spread_ref[:, pl.ds(at, SPAN)], NT)
        return 0

    lax.fori_loop(0, inputs // SPAN, merge, 0, unroll=4)
    picked_ref[...] = (merged_ref[...] * GRAD_SCALE).astype(BF16)

    group = GROUP
    chunk = group * tall
    quarter = width // REPS
    label_line = (
        lax.broadcasted_iota(jnp.int32, (chunk, group), 0)
        == lax.broadcasted_iota(jnp.int32, (chunk, group), 1) * tall + half
    ).astype(F32).astype(BF16)

    def place_rows(c, _):
        at = pl.multiple_of(c * chunk, chunk)
        doms = pl.ds(pl.multiple_of(c * group, group), group)
        place = lax.broadcasted_iota(jnp.int32, (chunk, uniq), 0) + at
        first_half = matmul(
            (target_ref[0:1, :] == place).astype(F32).astype(BF16), picked_ref[...]
        )
        second_half = matmul(
            (target_ref[1:2, :] == place).astype(F32).astype(BF16), picked_ref[...]
        )
        labels = matmul(label_line, high_ref[doms, :].astype(BF16)) * 16.0 + matmul(
            label_line, low_ref[doms, :].astype(BF16)
        )
        for r in range(REPS):
            columns = slice(r * quarter, (r + 1) * quarter)
            line = jnp.concatenate([first_half[:, columns], second_half[:, columns]], axis=1)
            out_ref[pl.ds(pl.multiple_of(r * domains * tall + at, 8), chunk), :] = line + labels
        return 0

    lax.fori_loop(0, domains // group, place_rows, 0)


def add_kernel(capacity, lines_ref, table_ref):
    half = capacity // 2
    tall = half + 1
    group = 64
    chunk = group * tall
    sources = lines_ref.shape[0] // tall
    quarter = LANES // 2
    height = table_ref.shape[0]

    def spot(shape, axis):
        index = lax.broadcasted_iota(jnp.int32, shape, axis)
        source = index // tall
        return source, index - source * tall

    def one(mask):
        return mask.astype(F32).astype(BF16)

    line_source, line_slot = spot((LANES, chunk), 1)
    lane = lax.broadcasted_iota(jnp.int32, (LANES, chunk), 0)
    real = line_slot < half
    spread_first = one((lane == line_slot) & real)
    spread_second = one((lane == line_slot + half) & real)
    mine = line_source[:group, :] == lax.broadcasted_iota(jnp.int32, (group, chunk), 0)
    col_source, _ = spot((chunk, group), 0)
    expand = one(col_source == lax.broadcasted_iota(jnp.int32, (chunk, group), 1))
    _, col_slot = spot((chunk, LANES), 0)
    col_lane = lax.broadcasted_iota(jnp.int32, (chunk, LANES), 1)
    col_real = col_slot < half
    at_first = (col_lane == col_slot) & col_real
    at_second = (col_lane == col_slot + half) & col_real
    left = col_lane < quarter
    place = lax.broadcasted_iota(jnp.int32, (height, chunk), 0)
    table_ref[...] = jnp.zeros(table_ref.shape, F32)

    def step(c, _):
        at = pl.multiple_of(c * chunk, 8)
        codes = lines_ref[pl.ds(at + half, group, stride=tall), :]
        lines = lines_ref[pl.ds(at, chunk), :]
        swapped = pltpu.roll(lines, quarter, 1)
        high = jnp.floor(codes * (1.0 / 16.0))
        low = (codes - high * 16.0).astype(BF16)
        high = high.astype(BF16)
        grown = matmul(expand, high) * 16.0 + matmul(expand, low)
        total = jnp.zeros(table_ref.shape, F32)
        for spread, at_column, pair in (
            (spread_first, at_first, jnp.where(left, lines, swapped)),
            (spread_second, at_second, jnp.where(left, swapped, lines)),
        ):
            flat = matmul(high, spread) * 16.0 + matmul(low, spread)
            row = jnp.sum(jnp.where(mine, flat, 0.0), axis=0, keepdims=True).astype(jnp.int32) - 1
            column = jnp.sum(jnp.where(at_column, grown, 0.0), axis=1, keepdims=True)
            column = column.astype(jnp.int32) - 1
            block = jnp.where(column < 0, -1, jnp.right_shift(column, 9))
            kept = [
                jnp.where(block == 2 * side + jnp.where(left, 0, 1), pair, 0.0).astype(BF16)
                for side in range(2)
            ]
            wide = jnp.concatenate(kept, axis=1)
            picker = one((row & (height - 1)) == place)
            total = total + matmul(picker, wide)
        table_ref[...] += total
        return 0

    lax.fori_loop(0, sources // group, step, 0)


def join_kernel(parts_ref, table_ref):
    height = parts_ref.shape[0] // REPS
    quarter = parts_ref.shape[1] // REPS
    for q in range(REPS):
        table_ref[q * height : (q + 1) * height, :] = jnp.concatenate(
            [
                parts_ref[r * height : (r + 1) * height, q * quarter : (q + 1) * quarter]
                for r in range(REPS)
            ],
            axis=1,
        )


VMEM = pl.BlockSpec(memory_space=pltpu.VMEM)
HBM = pl.BlockSpec(memory_space=pltpu.HBM)
PARAMS = pltpu.CompilerParams(vmem_limit_bytes=48 * 1024 * 1024)
LOCAL_PARAMS = pltpu.CompilerParams(vmem_limit_bytes=60 * 1024 * 1024)


def local_pass(capacity, domains, x, first, second, ids, owners, rows, cot, self1, agg1, self2, agg2):
    inputs, width = x.shape
    firsts = first.shape[1]
    uniq = owners.shape[1]
    arrays = (x, first, second, ids, owners, rows, cot, self1, agg1, self2, agg2)
    return pl.pallas_call(
        functools.partial(local_kernel, capacity),
        out_shape=(
            jax.ShapeDtypeStruct((REPS * domains * (capacity // 2 + 1), LANES), F32),
            jax.ShapeDtypeStruct((4 * width, width), F32),
        ),
        in_specs=[HBM] * 11,
        out_specs=(VMEM, VMEM),
        scratch_shapes=[
            pltpu.VMEM((width, inputs), BF16),
            pltpu.VMEM((inputs, firsts), BF16),
            pltpu.VMEM((width, firsts), BF16),
            pltpu.VMEM((width, firsts), BF16),
            pltpu.VMEM((width, firsts), F32),
            pltpu.VMEM((width, inputs), BF16),
            pltpu.VMEM((uniq, width), F32),
            pltpu.VMEM((uniq, width), BF16),
            pltpu.VMEM((2, uniq), jnp.int32),
            pltpu.VMEM((domains, LANES), F32),
            pltpu.VMEM((domains, LANES), F32),
            *[pltpu.VMEM(a.shape, a.dtype) for a in arrays],
            pltpu.SMEM(ids.shape, ids.dtype),
            pltpu.SemaphoreType.DMA((len(arrays) + 1,)),
        ],
        compiler_params=LOCAL_PARAMS,
        name="local_pass",
    )(*arrays)


def add_rows(capacity, lines):
    return pl.pallas_call(
        functools.partial(add_kernel, capacity),
        out_shape=jax.ShapeDtypeStruct((ROWS_OWN // REPS, 4 * (LANES // 2)), F32),
        in_specs=[VMEM],
        out_specs=VMEM,
        compiler_params=PARAMS,
        name="add_rows",
    )(lines)


def join_columns(parts):
    return pl.pallas_call(
        join_kernel,
        out_shape=jax.ShapeDtypeStruct(parts.shape, F32),
        in_specs=[VMEM],
        out_specs=VMEM,
        compiler_params=PARAMS,
        name="join_columns",
    )(parts)


def on_device(
    node_input,
    neighbor_first,
    neighbor_second,
    merge_ids,
    owner_ids,
    owner_rows,
    cotangent,
    self_first,
    agg_first,
    self_second,
    agg_second,
):
    target_total = cotangent.shape[0]
    width = node_input.shape[1]
    uniq_total = owner_rows.shape[0]
    domains = lax.axis_size("dom")
    factor = (domains * lax.axis_size("rep") * target_total) ** (-0.5)
    capacity = max(2, 5 * uniq_total // (4 * domains))
    outgoing, grads = local_pass(
        capacity,
        domains,
        node_input,
        neighbor_first.T,
        neighbor_second.T,
        merge_ids,
        owner_ids.T,
        owner_rows[None, :],
        cotangent,
        self_first,
        agg_first,
        self_second,
        agg_second,
    )
    arrived = lax.all_to_all(
        outgoing.reshape(REPS * domains, 1, -1), ("rep", "dom"), 0, 0, tiled=True
    )
    own_grads = lax.psum_scatter(grads, "rep", scatter_dimension=0, tiled=True)
    share = width // domains
    shares = lax.all_to_all(own_grads.reshape(domains, share, width), "dom", 0, 0, tiled=True)
    total = jnp.sum(shares, axis=0) * factor
    whole = lax.all_to_all(
        jnp.broadcast_to(total[None], (domains, share, width)), "dom", 0, 0, tiled=True
    ).reshape(width, width)
    arrived, whole = lax.optimization_barrier((arrived, whole))
    weight_grads = lax.all_to_all(
        jnp.broadcast_to(whole[None], (REPS, width, width)), "rep", 0, 0, tiled=True
    )
    quarter = add_rows(capacity, arrived.reshape(-1, LANES))
    table = join_columns(lax.all_gather(quarter, "rep", axis=0, tiled=True))
    return (table, weight_grads)


def solution(mesh):
    placed = (
        P(("dom", "rep"), None),
        P(("dom", "rep"), None),
        P(("dom", "rep"), None),
        P(("dom", "rep"), None),
        P(("dom", "rep"), None),
        P(("dom", "rep")),
        P(("dom", "rep"), None),
        P(),
        P(),
        P(),
        P(),
    )
    return jax.shard_map(
        on_device, mesh=mesh, in_specs=placed, out_specs=(P("dom", None), P()), check_vma=False
    )
```

```python
import functools

import jax
import jax.numpy as jnp
from jax import lax
from jax.experimental import pallas as pl
from jax.experimental.pallas import tpu as pltpu
from jax.sharding import PartitionSpec as P

ROWS_OWN = 2048
GRAD_SCALE = 16.0
NIBBLES = 8
DEPTH = 256
GROUP = 32
NIBBLE_BITS = 4
SPAN = 256
LANES = 128
REPS = 4
F32 = jnp.float32
BF16 = jnp.bfloat16
NN = (((1,), (0,)), ((), ()))
NT = (((1,), (1,)), ((), ()))


def matmul(a, b, dims=NN):
    return lax.dot_general(a, b, dims, preferred_element_type=F32)


def sigmoid(v):
    return 1.0 / (1.0 + jnp.exp(-v))


def local_kernel(
    capacity,
    x_hbm,
    first_hbm,
    second_hbm,
    ids_hbm,
    owners_hbm,
    rows_hbm,
    cot_hbm,
    self1_hbm,
    agg1_hbm,
    self2_hbm,
    agg2_hbm,
    out_ref,
    grads_ref,
    xt_ref,
    table_ref,
    mean_ref,
    down_ref,
    selfgrad_ref,
    spread_ref,
    merged_ref,
    picked_ref,
    target_ref,
    high_ref,
    low_ref,
    x_ref,
    first_ref,
    second_ref,
    ids_ref,
    owners_ref,
    rows_ref,
    cot_ref,
    self1_ref,
    agg1_ref,
    self2_ref,
    agg2_ref,
    ids_smem,
    sems,
):
    sources = (
        (owners_hbm, owners_ref),
        (rows_hbm, rows_ref),
        (first_hbm, first_ref),
        (x_hbm, x_ref),
        (second_hbm, second_ref),
        (cot_hbm, cot_ref),
        (self1_hbm, self1_ref),
        (agg1_hbm, agg1_ref),
        (self2_hbm, self2_ref),
        (agg2_hbm, agg2_ref),
        (ids_hbm, ids_ref),
        (ids_hbm, ids_smem),
    )
    copies = [
        pltpu.make_async_copy(source, local, sems.at[n])
        for n, (source, local) in enumerate(sources)
    ]
    for copy in copies:
        copy.start()

    inputs, width = x_ref.shape
    fan1, firsts = first_ref.shape
    fan2, batch = second_ref.shape
    uniq = owners_ref.shape[1]
    domains = high_ref.shape[0]
    words = inputs // NIBBLES
    lanes = 128
    depth = DEPTH
    turned = inputs // ((firsts // lanes) * (words // depth))

    copies[0].wait()
    copies[1].wait()
    upper = (
        lax.broadcasted_iota(jnp.int32, (SPAN, SPAN), 0)
        < lax.broadcasted_iota(jnp.int32, (SPAN, SPAN), 1)
    ).astype(BF16)
    domain = lax.broadcasted_iota(jnp.int32, (domains, SPAN), 0)
    half = capacity // 2
    tall = half + 1
    slot_place = lax.broadcasted_iota(jnp.int32, (LANES, SPAN), 0)
    carry = jnp.zeros((domains, 1), F32)
    high = jnp.zeros((domains, LANES), F32)
    low = jnp.zeros((domains, LANES), F32)
    for c in range(uniq // SPAN):
        at = c * SPAN
        owners = owners_ref[:, at : at + SPAN]
        marks = (owners == domain).astype(F32)
        marks_b = marks.astype(BF16)
        earlier = matmul(marks_b, upper) + carry
        slots = jnp.sum(earlier * marks, axis=0, keepdims=True).astype(jnp.int32)
        carry = carry + jnp.sum(marks, axis=1, keepdims=True)
        base = owners * tall + slots
        target_ref[0:1, at : at + SPAN] = jnp.where(slots < half, base, -1)
        target_ref[1:2, at : at + SPAN] = jnp.where(slots < half, -1, base - half)
        codes = rows_ref[:, at : at + SPAN] + 1
        here = slots == slot_place
        high = high + matmul(marks_b, jnp.where(here, codes // 16, 0).astype(F32).astype(BF16), NT)
        low = low + matmul(marks_b, jnp.where(here, codes % 16, 0).astype(F32).astype(BF16), NT)
    high_ref[...] = high
    low_ref[...] = low

    eye = (
        lax.broadcasted_iota(jnp.int32, (width, width), 0)
        == lax.broadcasted_iota(jnp.int32, (width, width), 1)
    ).astype(BF16)

    copies[2].wait()
    copies[3].wait()

    def count(step, _):
        col = pl.multiple_of((step // (words // depth)) * lanes, lanes)
        row = pl.multiple_of((step % (words // depth)) * depth, depth)
        nodes = first_ref[:, pl.ds(col, lanes)]
        keys = nodes % words
        values = jnp.left_shift(jnp.int32(1), (nodes // words) * NIBBLE_BITS)
        place = lax.broadcasted_iota(jnp.int32, (depth, lanes), 0) + row
        total = jnp.zeros((depth, lanes), jnp.int32)
        for k in range(fan1):
            total = total + jnp.where(keys[k : k + 1, :] == place, values[k : k + 1, :], 0)
        for part in range(NIBBLES):
            counts = jnp.bitwise_and(jnp.right_shift(total, part * NIBBLE_BITS), 15)
            table_ref[pl.ds(part * words + row, depth), pl.ds(col, lanes)] = counts.astype(
                F32
            ).astype(BF16)
        at = pl.multiple_of(step * turned, turned)
        xt_ref[:, pl.ds(at, turned)] = matmul(eye, x_ref[pl.ds(at, turned), :], NT).astype(BF16)
        return 0

    lax.fori_loop(0, (firsts // lanes) * (words // depth), count, 0, unroll=2)

    def mean(c, _):
        at = pl.multiple_of(c * SPAN, SPAN)
        mean_ref[:, pl.ds(at, SPAN)] = (
            matmul(xt_ref[...], table_ref[:, pl.ds(at, SPAN)]) / fan1
        ).astype(BF16)
        return 0

    lax.fori_loop(0, firsts // SPAN, mean, 0, unroll=2)

    for copy in copies[4:]:
        copy.wait()
    mean_one = mean_ref[...]
    selfs = xt_ref[:, :firsts]
    contract_first = (((0,), (0,)), ((), ()))
    preact = matmul(self1_ref[...], selfs, contract_first) + matmul(
        agg1_ref[...], mean_one, contract_first
    )
    gate = sigmoid(preact)
    hidden = (preact * gate).astype(BF16)
    second = jnp.zeros((firsts, batch), F32)
    place2 = lax.broadcasted_iota(jnp.int32, (firsts, batch), 0)
    for k in range(fan2):
        second = second + (second_ref[k : k + 1, :] == place2).astype(F32)
    second = second.astype(BF16)
    mean_two = (matmul(hidden, second) / fan2).astype(BF16)
    cot = cot_ref[...]
    grads_ref[2 * width : 3 * width, :] = matmul(hidden[:, :batch], cot)
    grads_ref[3 * width :, :] = matmul(mean_two, cot)
    down_two = (matmul(agg2_ref[...], cot, NT) / fan2).astype(BF16)
    hidden_grad = matmul(down_two, second, NT)
    targets_grad = hidden_grad[:, :batch] + matmul(self2_ref[...], cot, NT)
    hidden_grad = jnp.concatenate([targets_grad, hidden_grad[:, batch:]], axis=1)
    pre_grad = (hidden_grad * (gate * (1.0 + preact * (1.0 - gate)))).astype(BF16)
    grads_ref[:width, :] = matmul(selfs, pre_grad, NT)
    grads_ref[width : 2 * width, :] = matmul(mean_one, pre_grad, NT)
    down_ref[...] = (matmul(agg1_ref[...], pre_grad) / fan1).astype(BF16)
    selfgrad_ref[...] = matmul(self1_ref[...], pre_grad)

    step_rows = 512
    for c in range(firsts // step_rows):
        at = c * step_rows
        spread_ref[:, at : at + step_rows] = (
            matmul(down_ref[...], table_ref[at : at + step_rows, :], NT)
            + selfgrad_ref[:, at : at + step_rows]
        ).astype(BF16)

    def spread(c, _):
        at = pl.multiple_of(c * step_rows, step_rows)
        spread_ref[:, pl.ds(at, step_rows)] = matmul(
            down_ref[...], table_ref[pl.ds(at, step_rows), :], NT
        ).astype(BF16)
        return 0

    lax.fori_loop(firsts // step_rows, inputs // step_rows, spread, 0, unroll=2)

    window = SPAN + 8
    merged_ref[...] = jnp.zeros(merged_ref.shape, F32)

    def merge(c, _):
        at = pl.multiple_of(c * SPAN, SPAN)
        low = jnp.minimum(ids_smem[0, at] // 8, (uniq - window) // 8) * 8
        low = pl.multiple_of(low, 8)
        place = lax.broadcasted_iota(jnp.int32, (window, SPAN), 0) + low
        picker = (ids_ref[:, pl.ds(at, SPAN)] == place).astype(F32).astype(BF16)
        merged_ref[pl.ds(low, window), :] += matmul(picker, spread_ref[:, pl.ds(at, SPAN)], NT)
        return 0

    lax.fori_loop(0, inputs // SPAN, merge, 0, unroll=4)
    picked_ref[...] = (merged_ref[...] * GRAD_SCALE).astype(BF16)

    group = GROUP
    chunk = group * tall
    quarter = width // REPS
    label_line = (
        lax.broadcasted_iota(jnp.int32, (chunk, group), 0)
        == lax.broadcasted_iota(jnp.int32, (chunk, group), 1) * tall + half
    ).astype(F32).astype(BF16)

    def place_rows(c, _):
        at = pl.multiple_of(c * chunk, chunk)
        doms = pl.ds(pl.multiple_of(c * group, group), group)
        place = lax.broadcasted_iota(jnp.int32, (chunk, uniq), 0) + at
        first_half = matmul(
            (target_ref[0:1, :] == place).astype(F32).astype(BF16), picked_ref[...]
        )
        second_half = matmul(
            (target_ref[1:2, :] == place).astype(F32).astype(BF16), picked_ref[...]
        )
        labels = matmul(label_line, high_ref[doms, :].astype(BF16)) * 16.0 + matmul(
            label_line, low_ref[doms, :].astype(BF16)
        )
        for r in range(REPS):
            columns = slice(r * quarter, (r + 1) * quarter)
            line = jnp.concatenate([first_half[:, columns], second_half[:, columns]], axis=1)
            out_ref[pl.ds(pl.multiple_of(r * domains * tall + at, 8), chunk), :] = line + labels
        return 0

    lax.fori_loop(0, domains // group, place_rows, 0)


def add_kernel(capacity, lines_ref, table_ref):
    half = capacity // 2
    tall = half + 1
    group = 64
    chunk = group * tall
    sources = lines_ref.shape[0] // tall
    quarter = LANES // 2
    height = table_ref.shape[0]

    def spot(shape, axis):
        index = lax.broadcasted_iota(jnp.int32, shape, axis)
        source = index // tall
        return source, index - source * tall

    def one(mask):
        return mask.astype(F32).astype(BF16)

    line_source, line_slot = spot((LANES, chunk), 1)
    lane = lax.broadcasted_iota(jnp.int32, (LANES, chunk), 0)
    real = line_slot < half
    spread_first = one((lane == line_slot) & real)
    spread_second = one((lane == line_slot + half) & real)
    mine = line_source[:group, :] == lax.broadcasted_iota(jnp.int32, (group, chunk), 0)
    col_source, _ = spot((chunk, group), 0)
    expand = one(col_source == lax.broadcasted_iota(jnp.int32, (chunk, group), 1))
    _, col_slot = spot((chunk, LANES), 0)
    col_lane = lax.broadcasted_iota(jnp.int32, (chunk, LANES), 1)
    col_real = col_slot < half
    at_first = (col_lane == col_slot) & col_real
    at_second = (col_lane == col_slot + half) & col_real
    left = col_lane < quarter
    place = lax.broadcasted_iota(jnp.int32, (height, chunk), 0)
    table_ref[...] = jnp.zeros(table_ref.shape, F32)

    def step(c, _):
        at = pl.multiple_of(c * chunk, 8)
        codes = lines_ref[pl.ds(at + half, group, stride=tall), :]
        lines = lines_ref[pl.ds(at, chunk), :]
        swapped = pltpu.roll(lines, quarter, 1)
        high = jnp.floor(codes * (1.0 / 16.0))
        low = (codes - high * 16.0).astype(BF16)
        high = high.astype(BF16)
        grown = matmul(expand, high) * 16.0 + matmul(expand, low)
        total = jnp.zeros(table_ref.shape, F32)
        for spread, at_column, pair in (
            (spread_first, at_first, jnp.where(left, lines, swapped)),
            (spread_second, at_second, jnp.where(left, swapped, lines)),
        ):
            flat = matmul(high, spread) * 16.0 + matmul(low, spread)
            row = jnp.sum(jnp.where(mine, flat, 0.0), axis=0, keepdims=True).astype(jnp.int32) - 1
            column = jnp.sum(jnp.where(at_column, grown, 0.0), axis=1, keepdims=True)
            column = column.astype(jnp.int32) - 1
            block = jnp.where(column < 0, -1, jnp.right_shift(column, 9))
            kept = [
                jnp.where(block == 2 * side + jnp.where(left, 0, 1), pair, 0.0).astype(BF16)
                for side in range(2)
            ]
            wide = jnp.concatenate(kept, axis=1)
            picker = one((row & (height - 1)) == place)
            total = total + matmul(picker, wide)
        table_ref[...] += total
        return 0

    lax.fori_loop(0, sources // group, step, 0)


def join_kernel(parts_ref, table_ref):
    height = parts_ref.shape[0] // REPS
    quarter = parts_ref.shape[1] // REPS
    for q in range(REPS):
        table_ref[q * height : (q + 1) * height, :] = jnp.concatenate(
            [
                parts_ref[r * height : (r + 1) * height, q * quarter : (q + 1) * quarter]
                for r in range(REPS)
            ],
            axis=1,
        )


VMEM = pl.BlockSpec(memory_space=pltpu.VMEM)
HBM = pl.BlockSpec(memory_space=pltpu.HBM)
PARAMS = pltpu.CompilerParams(vmem_limit_bytes=48 * 1024 * 1024)
LOCAL_PARAMS = pltpu.CompilerParams(vmem_limit_bytes=60 * 1024 * 1024)


def local_pass(capacity, domains, x, first, second, ids, owners, rows, cot, self1, agg1, self2, agg2):
    inputs, width = x.shape
    firsts = first.shape[1]
    uniq = owners.shape[1]
    arrays = (x, first, second, ids, owners, rows, cot, self1, agg1, self2, agg2)
    return pl.pallas_call(
        functools.partial(local_kernel, capacity),
        out_shape=(
            jax.ShapeDtypeStruct((REPS * domains * (capacity // 2 + 1), LANES), F32),
            jax.ShapeDtypeStruct((4 * width, width), F32),
        ),
        in_specs=[HBM] * 11,
        out_specs=(VMEM, VMEM),
        scratch_shapes=[
            pltpu.VMEM((width, inputs), BF16),
            pltpu.VMEM((inputs, firsts), BF16),
            pltpu.VMEM((width, firsts), BF16),
            pltpu.VMEM((width, firsts), BF16),
            pltpu.VMEM((width, firsts), F32),
            pltpu.VMEM((width, inputs), BF16),
            pltpu.VMEM((uniq, width), F32),
            pltpu.VMEM((uniq, width), BF16),
            pltpu.VMEM((2, uniq), jnp.int32),
            pltpu.VMEM((domains, LANES), F32),
            pltpu.VMEM((domains, LANES), F32),
            *[pltpu.VMEM(a.shape, a.dtype) for a in arrays],
            pltpu.SMEM(ids.shape, ids.dtype),
            pltpu.SemaphoreType.DMA((len(arrays) + 1,)),
        ],
        compiler_params=LOCAL_PARAMS,
        name="local_pass",
    )(*arrays)


def add_rows(capacity, lines):
    return pl.pallas_call(
        functools.partial(add_kernel, capacity),
        out_shape=jax.ShapeDtypeStruct((ROWS_OWN // REPS, 4 * (LANES // 2)), F32),
        in_specs=[VMEM],
        out_specs=VMEM,
        compiler_params=PARAMS,
        name="add_rows",
    )(lines)


def join_columns(parts):
    return pl.pallas_call(
        join_kernel,
        out_shape=jax.ShapeDtypeStruct(parts.shape, F32),
        in_specs=[VMEM],
        out_specs=VMEM,
        compiler_params=PARAMS,
        name="join_columns",
    )(parts)


def sum_over_domains(value, domains):
    place = lax.axis_index("dom")
    steps = [1 << bit for bit in range(domains.bit_length() - 1)]

    def swap(part, step):
        return lax.ppermute(part, "dom", [(i, i ^ step) for i in range(domains)])

    for step in steps:
        pairs = value.reshape(value.shape[0] // 2, 2, *value.shape[1:])
        upper = (place & step) != 0
        sent = jnp.where(upper, pairs[:, 0], pairs[:, 1])
        kept = jnp.where(upper, pairs[:, 1], pairs[:, 0])
        value = kept + swap(sent, step)
    return value[0]


def on_device(
    node_input,
    neighbor_first,
    neighbor_second,
    merge_ids,
    owner_ids,
    owner_rows,
    cotangent,
    self_first,
    agg_first,
    self_second,
    agg_second,
):
    target_total = cotangent.shape[0]
    width = node_input.shape[1]
    uniq_total = owner_rows.shape[0]
    domains = lax.axis_size("dom")
    factor = (domains * lax.axis_size("rep") * target_total) ** (-0.5)
    capacity = max(2, 5 * uniq_total // (4 * domains))
    outgoing, grads = local_pass(
        capacity,
        domains,
        node_input,
        neighbor_first.T,
        neighbor_second.T,
        merge_ids,
        owner_ids.T,
        owner_rows[None, :],
        cotangent,
        self_first,
        agg_first,
        self_second,
        agg_second,
    )
    arrived = lax.all_to_all(
        outgoing.reshape(REPS * domains, 1, -1), ("rep", "dom"), 0, 0, tiled=True
    )
    own_grads = lax.psum_scatter(grads, "rep", scatter_dimension=0, tiled=True)
    share = width // domains
    total = sum_over_domains(own_grads.reshape(domains, share, width), domains) * factor
    arrived, total = lax.optimization_barrier((arrived, total))
    whole = lax.all_to_all(
        jnp.broadcast_to(total[None], (domains, share, width)), "dom", 0, 0, tiled=True
    ).reshape(width, width)
    weight_grads = lax.all_to_all(
        jnp.broadcast_to(whole[None], (REPS, width, width)), "rep", 0, 0, tiled=True
    )
    quarter = add_rows(capacity, arrived.reshape(-1, LANES))
    table = join_columns(lax.all_gather(quarter, "rep", axis=0, tiled=True))
    return (table, weight_grads)


def solution(mesh):
    placed = (
        P(("dom", "rep"), None),
        P(("dom", "rep"), None),
        P(("dom", "rep"), None),
        P(("dom", "rep"), None),
        P(("dom", "rep"), None),
        P(("dom", "rep")),
        P(("dom", "rep"), None),
        P(),
        P(),
        P(),
        P(),
    )
    return jax.shard_map(
        on_device, mesh=mesh, in_specs=placed, out_specs=(P("dom", None), P()), check_vma=False
    )
```

```python
import functools

import jax
import jax.numpy as jnp
from jax import lax
from jax.experimental import pallas as pl
from jax.experimental.pallas import tpu as pltpu
from jax.sharding import PartitionSpec as P

ROWS_OWN = 2048
GRAD_SCALE = 16.0
NIBBLES = 8
DEPTH = 256
GROUP = 32
NIBBLE_BITS = 4
SPAN = 256
LANES = 128
REPS = 4
F32 = jnp.float32
BF16 = jnp.bfloat16
NN = (((1,), (0,)), ((), ()))
NT = (((1,), (1,)), ((), ()))


def matmul(a, b, dims=NN):
    return lax.dot_general(a, b, dims, preferred_element_type=F32)


def sigmoid(v):
    return 1.0 / (1.0 + jnp.exp(-v))


def local_kernel(
    capacity,
    x_hbm,
    first_hbm,
    second_hbm,
    ids_hbm,
    owners_hbm,
    rows_hbm,
    cot_hbm,
    self1_hbm,
    agg1_hbm,
    self2_hbm,
    agg2_hbm,
    out_ref,
    grads_ref,
    xt_ref,
    table_ref,
    mean_ref,
    down_ref,
    selfgrad_ref,
    spread_ref,
    merged_ref,
    picked_ref,
    target_ref,
    high_ref,
    low_ref,
    x_ref,
    first_ref,
    second_ref,
    ids_ref,
    owners_ref,
    rows_ref,
    cot_ref,
    self1_ref,
    agg1_ref,
    self2_ref,
    agg2_ref,
    ids_smem,
    sems,
):
    sources = (
        (owners_hbm, owners_ref),
        (rows_hbm, rows_ref),
        (first_hbm, first_ref),
        (x_hbm, x_ref),
        (second_hbm, second_ref),
        (cot_hbm, cot_ref),
        (self1_hbm, self1_ref),
        (agg1_hbm, agg1_ref),
        (self2_hbm, self2_ref),
        (agg2_hbm, agg2_ref),
        (ids_hbm, ids_ref),
        (ids_hbm, ids_smem),
    )
    copies = [
        pltpu.make_async_copy(source, local, sems.at[n])
        for n, (source, local) in enumerate(sources)
    ]
    for copy in copies:
        copy.start()

    inputs, width = x_ref.shape
    fan1, firsts = first_ref.shape
    fan2, batch = second_ref.shape
    uniq = owners_ref.shape[1]
    domains = high_ref.shape[0]
    words = inputs // NIBBLES
    lanes = 128
    depth = DEPTH
    turned = inputs // ((firsts // lanes) * (words // depth))

    copies[0].wait()
    copies[1].wait()
    upper = (
        lax.broadcasted_iota(jnp.int32, (SPAN, SPAN), 0)
        < lax.broadcasted_iota(jnp.int32, (SPAN, SPAN), 1)
    ).astype(BF16)
    domain = lax.broadcasted_iota(jnp.int32, (domains, SPAN), 0)
    half = capacity // 2
    tall = half + 1
    slot_place = lax.broadcasted_iota(jnp.int32, (LANES, SPAN), 0)
    carry = jnp.zeros((domains, 1), F32)
    high = jnp.zeros((domains, LANES), F32)
    low = jnp.zeros((domains, LANES), F32)
    for c in range(uniq // SPAN):
        at = c * SPAN
        owners = owners_ref[:, at : at + SPAN]
        marks = (owners == domain).astype(F32)
        marks_b = marks.astype(BF16)
        earlier = matmul(marks_b, upper) + carry
        slots = jnp.sum(earlier * marks, axis=0, keepdims=True).astype(jnp.int32)
        carry = carry + jnp.sum(marks, axis=1, keepdims=True)
        base = owners * tall + slots
        target_ref[0:1, at : at + SPAN] = jnp.where(slots < half, base, -1)
        target_ref[1:2, at : at + SPAN] = jnp.where(slots < half, -1, base - half)
        codes = rows_ref[:, at : at + SPAN] + 1
        here = slots == slot_place
        high = high + matmul(marks_b, jnp.where(here, codes // 16, 0).astype(F32).astype(BF16), NT)
        low = low + matmul(marks_b, jnp.where(here, codes % 16, 0).astype(F32).astype(BF16), NT)
    high_ref[...] = high
    low_ref[...] = low

    eye = (
        lax.broadcasted_iota(jnp.int32, (width, width), 0)
        == lax.broadcasted_iota(jnp.int32, (width, width), 1)
    ).astype(BF16)

    copies[2].wait()
    copies[3].wait()

    def count(step, _):
        col = pl.multiple_of((step // (words // depth)) * lanes, lanes)
        row = pl.multiple_of((step % (words // depth)) * depth, depth)
        nodes = first_ref[:, pl.ds(col, lanes)]
        keys = nodes % words
        values = jnp.left_shift(jnp.int32(1), (nodes // words) * NIBBLE_BITS)
        place = lax.broadcasted_iota(jnp.int32, (depth, lanes), 0) + row
        total = jnp.zeros((depth, lanes), jnp.int32)
        for k in range(fan1):
            total = total + jnp.where(keys[k : k + 1, :] == place, values[k : k + 1, :], 0)
        for part in range(NIBBLES):
            counts = jnp.bitwise_and(jnp.right_shift(total, part * NIBBLE_BITS), 15)
            table_ref[pl.ds(part * words + row, depth), pl.ds(col, lanes)] = counts.astype(
                F32
            ).astype(BF16)
        at = pl.multiple_of(step * turned, turned)
        xt_ref[:, pl.ds(at, turned)] = matmul(eye, x_ref[pl.ds(at, turned), :], NT).astype(BF16)
        return 0

    lax.fori_loop(0, (firsts // lanes) * (words // depth), count, 0, unroll=2)

    def mean(c, _):
        at = pl.multiple_of(c * SPAN, SPAN)
        mean_ref[:, pl.ds(at, SPAN)] = (
            matmul(xt_ref[...], table_ref[:, pl.ds(at, SPAN)]) / fan1
        ).astype(BF16)
        return 0

    lax.fori_loop(0, firsts // SPAN, mean, 0, unroll=2)

    for copy in copies[4:]:
        copy.wait()
    mean_one = mean_ref[...]
    selfs = xt_ref[:, :firsts]
    contract_first = (((0,), (0,)), ((), ()))
    preact = matmul(self1_ref[...], selfs, contract_first) + matmul(
        agg1_ref[...], mean_one, contract_first
    )
    gate = sigmoid(preact)
    hidden = (preact * gate).astype(BF16)
    second = jnp.zeros((firsts, batch), F32)
    place2 = lax.broadcasted_iota(jnp.int32, (firsts, batch), 0)
    for k in range(fan2):
        second = second + (second_ref[k : k + 1, :] == place2).astype(F32)
    second = second.astype(BF16)
    mean_two = (matmul(hidden, second) / fan2).astype(BF16)
    cot = cot_ref[...]
    grads_ref[2 * width : 3 * width, :] = matmul(hidden[:, :batch], cot)
    grads_ref[3 * width :, :] = matmul(mean_two, cot)
    down_two = (matmul(agg2_ref[...], cot, NT) / fan2).astype(BF16)
    hidden_grad = matmul(down_two, second, NT)
    targets_grad = hidden_grad[:, :batch] + matmul(self2_ref[...], cot, NT)
    hidden_grad = jnp.concatenate([targets_grad, hidden_grad[:, batch:]], axis=1)
    pre_grad = (hidden_grad * (gate * (1.0 + preact * (1.0 - gate)))).astype(BF16)
    grads_ref[:width, :] = matmul(selfs, pre_grad, NT)
    grads_ref[width : 2 * width, :] = matmul(mean_one, pre_grad, NT)
    down_ref[...] = (matmul(agg1_ref[...], pre_grad) / fan1).astype(BF16)
    selfgrad_ref[...] = matmul(self1_ref[...], pre_grad)

    step_rows = 512
    for c in range(firsts // step_rows):
        at = c * step_rows
        spread_ref[:, at : at + step_rows] = (
            matmul(down_ref[...], table_ref[at : at + step_rows, :], NT)
            + selfgrad_ref[:, at : at + step_rows]
        ).astype(BF16)

    def spread(c, _):
        at = pl.multiple_of(c * step_rows, step_rows)
        spread_ref[:, pl.ds(at, step_rows)] = matmul(
            down_ref[...], table_ref[pl.ds(at, step_rows), :], NT
        ).astype(BF16)
        return 0

    lax.fori_loop(firsts // step_rows, inputs // step_rows, spread, 0, unroll=2)

    window = SPAN + 8
    merged_ref[...] = jnp.zeros(merged_ref.shape, F32)

    def merge(c, _):
        at = pl.multiple_of(c * SPAN, SPAN)
        low = jnp.minimum(ids_smem[0, at] // 8, (uniq - window) // 8) * 8
        low = pl.multiple_of(low, 8)
        place = lax.broadcasted_iota(jnp.int32, (window, SPAN), 0) + low
        picker = (ids_ref[:, pl.ds(at, SPAN)] == place).astype(F32).astype(BF16)
        merged_ref[pl.ds(low, window), :] += matmul(picker, spread_ref[:, pl.ds(at, SPAN)], NT)
        return 0

    lax.fori_loop(0, inputs // SPAN, merge, 0, unroll=4)
    picked_ref[...] = (merged_ref[...] * GRAD_SCALE).astype(BF16)

    group = GROUP
    chunk = group * tall
    quarter = width // REPS
    label_line = (
        lax.broadcasted_iota(jnp.int32, (chunk, group), 0)
        == lax.broadcasted_iota(jnp.int32, (chunk, group), 1) * tall + half
    ).astype(F32).astype(BF16)

    def place_rows(c, _):
        at = pl.multiple_of(c * chunk, chunk)
        doms = pl.ds(pl.multiple_of(c * group, group), group)
        place = lax.broadcasted_iota(jnp.int32, (chunk, uniq), 0) + at
        first_half = matmul(
            (target_ref[0:1, :] == place).astype(F32).astype(BF16), picked_ref[...]
        )
        second_half = matmul(
            (target_ref[1:2, :] == place).astype(F32).astype(BF16), picked_ref[...]
        )
        labels = matmul(label_line, high_ref[doms, :].astype(BF16)) * 16.0 + matmul(
            label_line, low_ref[doms, :].astype(BF16)
        )
        for r in range(REPS):
            columns = slice(r * quarter, (r + 1) * quarter)
            line = jnp.concatenate([first_half[:, columns], second_half[:, columns]], axis=1)
            out_ref[pl.ds(pl.multiple_of(r * domains * tall + at, 8), chunk), :] = line + labels
        return 0

    lax.fori_loop(0, domains // group, place_rows, 0)


def add_kernel(capacity, lines_ref, table_ref):
    half = capacity // 2
    tall = half + 1
    sources = lines_ref.shape[0] // tall
    quarter = LANES // 2
    height = table_ref.shape[0]
    codes = lines_ref[pl.ds(half, sources, stride=tall), :]
    rows = codes.T.astype(jnp.int32) - 1
    blocks = jnp.right_shift(codes.astype(jnp.int32) - 1, height.bit_length() - 1)
    rows = jnp.where(rows < 0, -1, rows & (height - 1))
    left = lax.broadcasted_iota(jnp.int32, (sources, LANES), 1) < quarter
    sides = [jnp.where(left, 0, 1) + 2 * side for side in range(2)]
    place = lax.broadcasted_iota(jnp.int32, (height, sources), 0)
    table_ref[...] = jnp.zeros(table_ref.shape, F32)
    together = 5
    for start in range(0, half, together):
        pickers, wides = [], []
        for slot in range(start, min(start + together, half)):
            lines = lines_ref[pl.ds(slot, sources, stride=tall), :]
            swapped = pltpu.roll(lines, quarter, 1)
            for at, pair in (
                (slot, jnp.where(left, lines, swapped)),
                (slot + half, jnp.where(left, swapped, lines)),
            ):
                block = blocks[:, at : at + 1]
                kept = [jnp.where(block == side, pair, 0.0).astype(BF16) for side in sides]
                wides.append(jnp.concatenate(kept, axis=1))
                pickers.append((rows[at : at + 1, :] == place).astype(F32).astype(BF16))
        table_ref[...] += matmul(
            jnp.concatenate(pickers, axis=1), jnp.concatenate(wides, axis=0)
        )


def join_kernel(parts_ref, table_ref):
    height = parts_ref.shape[0] // REPS
    quarter = parts_ref.shape[1] // REPS
    for q in range(REPS):
        table_ref[q * height : (q + 1) * height, :] = jnp.concatenate(
            [
                parts_ref[r * height : (r + 1) * height, q * quarter : (q + 1) * quarter]
                for r in range(REPS)
            ],
            axis=1,
        )


VMEM = pl.BlockSpec(memory_space=pltpu.VMEM)
HBM = pl.BlockSpec(memory_space=pltpu.HBM)
PARAMS = pltpu.CompilerParams(vmem_limit_bytes=48 * 1024 * 1024)
LOCAL_PARAMS = pltpu.CompilerParams(vmem_limit_bytes=60 * 1024 * 1024)


def local_pass(capacity, domains, x, first, second, ids, owners, rows, cot, self1, agg1, self2, agg2):
    inputs, width = x.shape
    firsts = first.shape[1]
    uniq = owners.shape[1]
    arrays = (x, first, second, ids, owners, rows, cot, self1, agg1, self2, agg2)
    return pl.pallas_call(
        functools.partial(local_kernel, capacity),
        out_shape=(
            jax.ShapeDtypeStruct((REPS * domains * (capacity // 2 + 1), LANES), F32),
            jax.ShapeDtypeStruct((4 * width, width), F32),
        ),
        in_specs=[HBM] * 11,
        out_specs=(VMEM, VMEM),
        scratch_shapes=[
            pltpu.VMEM((width, inputs), BF16),
            pltpu.VMEM((inputs, firsts), BF16),
            pltpu.VMEM((width, firsts), BF16),
            pltpu.VMEM((width, firsts), BF16),
            pltpu.VMEM((width, firsts), F32),
            pltpu.VMEM((width, inputs), BF16),
            pltpu.VMEM((uniq, width), F32),
            pltpu.VMEM((uniq, width), BF16),
            pltpu.VMEM((2, uniq), jnp.int32),
            pltpu.VMEM((domains, LANES), F32),
            pltpu.VMEM((domains, LANES), F32),
            *[pltpu.VMEM(a.shape, a.dtype) for a in arrays],
            pltpu.SMEM(ids.shape, ids.dtype),
            pltpu.SemaphoreType.DMA((len(arrays) + 1,)),
        ],
        compiler_params=LOCAL_PARAMS,
        name="local_pass",
    )(*arrays)


def add_rows(capacity, lines):
    return pl.pallas_call(
        functools.partial(add_kernel, capacity),
        out_shape=jax.ShapeDtypeStruct((ROWS_OWN // REPS, 4 * (LANES // 2)), F32),
        in_specs=[VMEM],
        out_specs=VMEM,
        compiler_params=PARAMS,
        name="add_rows",
    )(lines)


def join_columns(parts):
    return pl.pallas_call(
        join_kernel,
        out_shape=jax.ShapeDtypeStruct(parts.shape, F32),
        in_specs=[VMEM],
        out_specs=VMEM,
        compiler_params=PARAMS,
        name="join_columns",
    )(parts)


def sum_over_domains(value, domains):
    place = lax.axis_index("dom")
    steps = [1 << bit for bit in range(domains.bit_length() - 1)]

    def swap(part, step):
        return lax.ppermute(part, "dom", [(i, i ^ step) for i in range(domains)])

    for step in steps:
        pairs = value.reshape(value.shape[0] // 2, 2, *value.shape[1:])
        upper = (place & step) != 0
        sent = jnp.where(upper, pairs[:, 0], pairs[:, 1])
        kept = jnp.where(upper, pairs[:, 1], pairs[:, 0])
        value = kept + swap(sent, step)
    return value[0]


def on_device(
    node_input,
    neighbor_first,
    neighbor_second,
    merge_ids,
    owner_ids,
    owner_rows,
    cotangent,
    self_first,
    agg_first,
    self_second,
    agg_second,
):
    target_total = cotangent.shape[0]
    width = node_input.shape[1]
    uniq_total = owner_rows.shape[0]
    domains = lax.axis_size("dom")
    factor = (domains * lax.axis_size("rep") * target_total) ** (-0.5)
    capacity = max(2, 5 * uniq_total // (4 * domains))
    outgoing, grads = local_pass(
        capacity,
        domains,
        node_input,
        neighbor_first.T,
        neighbor_second.T,
        merge_ids,
        owner_ids.T,
        owner_rows[None, :],
        cotangent,
        self_first,
        agg_first,
        self_second,
        agg_second,
    )
    arrived = lax.all_to_all(
        outgoing.reshape(REPS * domains, 1, -1), ("rep", "dom"), 0, 0, tiled=True
    )
    own_grads = lax.psum_scatter(grads, "rep", scatter_dimension=0, tiled=True)
    share = width // domains
    total = sum_over_domains(own_grads.reshape(domains, share, width), domains) * factor
    arrived, total = lax.optimization_barrier((arrived, total))
    whole = lax.all_to_all(
        jnp.broadcast_to(total[None], (domains, share, width)), "dom", 0, 0, tiled=True
    ).reshape(width, width)
    place = lax.axis_index("rep")
    parts = [whole] + [
        lax.ppermute(whole, "rep", [(i, (i + step) % REPS) for i in range(REPS)])
        for step in range(1, REPS)
    ]
    weight_grads = jnp.stack(
        [
            jnp.where(
                place == matrix,
                parts[0],
                jnp.where(
                    place == (matrix + 1) % REPS,
                    parts[1],
                    jnp.where(place == (matrix + 2) % REPS, parts[2], parts[3]),
                ),
            )
            for matrix in range(REPS)
        ]
    )
    quarter = add_rows(capacity, arrived.reshape(-1, LANES))
    table = join_columns(lax.all_gather(quarter, "rep", axis=0, tiled=True))
    return (table, weight_grads)


def solution(mesh):
    placed = (
        P(("dom", "rep"), None),
        P(("dom", "rep"), None),
        P(("dom", "rep"), None),
        P(("dom", "rep"), None),
        P(("dom", "rep"), None),
        P(("dom", "rep")),
        P(("dom", "rep"), None),
        P(),
        P(),
        P(),
        P(),
    )
    return jax.shard_map(
        on_device, mesh=mesh, in_specs=placed, out_specs=(P("dom", None), P()), check_vma=False
    )
```

```python
import functools

import jax
import jax.numpy as jnp
from jax import lax
from jax.experimental import pallas as pl
from jax.experimental.pallas import tpu as pltpu
from jax.sharding import PartitionSpec as P

ROWS_OWN = 2048
GRAD_SCALE = 16.0
NIBBLES = 8
DEPTH = 256
GROUP = 32
NIBBLE_BITS = 4
SPAN = 256
LANES = 128
REPS = 4
F32 = jnp.float32
BF16 = jnp.bfloat16
NN = (((1,), (0,)), ((), ()))
NT = (((1,), (1,)), ((), ()))


def matmul(a, b, dims=NN):
    return lax.dot_general(a, b, dims, preferred_element_type=F32)


def sigmoid(v):
    return 1.0 / (1.0 + jnp.exp(-v))


def local_kernel(
    capacity,
    x_hbm,
    first_hbm,
    second_hbm,
    ids_hbm,
    owners_hbm,
    rows_hbm,
    cot_hbm,
    self1_hbm,
    agg1_hbm,
    self2_hbm,
    agg2_hbm,
    out_ref,
    grads_ref,
    xt_ref,
    table_ref,
    mean_ref,
    down_ref,
    selfgrad_ref,
    spread_ref,
    merged_ref,
    picked_ref,
    target_ref,
    high_ref,
    low_ref,
    x_ref,
    first_ref,
    second_ref,
    ids_ref,
    owners_ref,
    rows_ref,
    cot_ref,
    self1_ref,
    agg1_ref,
    self2_ref,
    agg2_ref,
    ids_smem,
    sems,
):
    sources = (
        (owners_hbm, owners_ref),
        (rows_hbm, rows_ref),
        (first_hbm, first_ref),
        (x_hbm, x_ref),
        (second_hbm, second_ref),
        (cot_hbm, cot_ref),
        (self1_hbm, self1_ref),
        (agg1_hbm, agg1_ref),
        (self2_hbm, self2_ref),
        (agg2_hbm, agg2_ref),
        (ids_hbm, ids_ref),
        (ids_hbm, ids_smem),
    )
    copies = [
        pltpu.make_async_copy(source, local, sems.at[n])
        for n, (source, local) in enumerate(sources)
    ]
    for copy in copies:
        copy.start()

    inputs, width = x_ref.shape
    fan1, firsts = first_ref.shape
    fan2, batch = second_ref.shape
    uniq = owners_ref.shape[1]
    domains = high_ref.shape[0]
    words = inputs // NIBBLES
    lanes = 128
    depth = DEPTH
    turned = inputs // ((firsts // lanes) * (words // depth))

    copies[0].wait()
    copies[1].wait()
    upper = (
        lax.broadcasted_iota(jnp.int32, (SPAN, SPAN), 0)
        < lax.broadcasted_iota(jnp.int32, (SPAN, SPAN), 1)
    ).astype(BF16)
    domain = lax.broadcasted_iota(jnp.int32, (domains, SPAN), 0)
    half = capacity // 2
    tall = half + 1
    slot_place = lax.broadcasted_iota(jnp.int32, (LANES, SPAN), 0)
    carry = jnp.zeros((domains, 1), F32)
    high = jnp.zeros((domains, LANES), F32)
    low = jnp.zeros((domains, LANES), F32)
    for c in range(uniq // SPAN):
        at = c * SPAN
        owners = owners_ref[:, at : at + SPAN]
        marks = (owners == domain).astype(F32)
        marks_b = marks.astype(BF16)
        earlier = matmul(marks_b, upper) + carry
        slots = jnp.sum(earlier * marks, axis=0, keepdims=True).astype(jnp.int32)
        carry = carry + jnp.sum(marks, axis=1, keepdims=True)
        base = owners * tall + slots
        target_ref[0:1, at : at + SPAN] = jnp.where(slots < half, base, -1)
        target_ref[1:2, at : at + SPAN] = jnp.where(slots < half, -1, base - half)
        codes = rows_ref[:, at : at + SPAN] + 1
        here = slots == slot_place
        high = high + matmul(marks_b, jnp.where(here, codes // 16, 0).astype(F32).astype(BF16), NT)
        low = low + matmul(marks_b, jnp.where(here, codes % 16, 0).astype(F32).astype(BF16), NT)
    high_ref[...] = high
    low_ref[...] = low

    eye = (
        lax.broadcasted_iota(jnp.int32, (width, width), 0)
        == lax.broadcasted_iota(jnp.int32, (width, width), 1)
    ).astype(BF16)

    copies[2].wait()
    copies[3].wait()

    def count(step, _):
        col = pl.multiple_of((step // (words // depth)) * lanes, lanes)
        row = pl.multiple_of((step % (words // depth)) * depth, depth)
        nodes = first_ref[:, pl.ds(col, lanes)]
        keys = nodes % words
        values = jnp.left_shift(jnp.int32(1), (nodes // words) * NIBBLE_BITS)
        place = lax.broadcasted_iota(jnp.int32, (depth, lanes), 0) + row
        total = jnp.zeros((depth, lanes), jnp.int32)
        for k in range(fan1):
            total = total + jnp.where(keys[k : k + 1, :] == place, values[k : k + 1, :], 0)
        for part in range(NIBBLES):
            counts = jnp.bitwise_and(jnp.right_shift(total, part * NIBBLE_BITS), 15)
            table_ref[pl.ds(part * words + row, depth), pl.ds(col, lanes)] = counts.astype(
                F32
            ).astype(BF16)
        at = pl.multiple_of(step * turned, turned)
        xt_ref[:, pl.ds(at, turned)] = matmul(eye, x_ref[pl.ds(at, turned), :], NT).astype(BF16)
        return 0

    lax.fori_loop(0, (firsts // lanes) * (words // depth), count, 0, unroll=2)

    def mean(c, _):
        at = pl.multiple_of(c * SPAN, SPAN)
        mean_ref[:, pl.ds(at, SPAN)] = (
            matmul(xt_ref[...], table_ref[:, pl.ds(at, SPAN)]) / fan1
        ).astype(BF16)
        return 0

    lax.fori_loop(0, firsts // SPAN, mean, 0, unroll=2)

    for copy in copies[4:]:
        copy.wait()
    mean_one = mean_ref[...]
    selfs = xt_ref[:, :firsts]
    contract_first = (((0,), (0,)), ((), ()))
    preact = matmul(self1_ref[...], selfs, contract_first) + matmul(
        agg1_ref[...], mean_one, contract_first
    )
    gate = sigmoid(preact)
    hidden = (preact * gate).astype(BF16)
    second = jnp.zeros((firsts, batch), F32)
    place2 = lax.broadcasted_iota(jnp.int32, (firsts, batch), 0)
    for k in range(fan2):
        second = second + (second_ref[k : k + 1, :] == place2).astype(F32)
    second = second.astype(BF16)
    mean_two = (matmul(hidden, second) / fan2).astype(BF16)
    cot = cot_ref[...]
    grads_ref[2 * width : 3 * width, :] = matmul(hidden[:, :batch], cot)
    grads_ref[3 * width :, :] = matmul(mean_two, cot)
    down_two = (matmul(agg2_ref[...], cot, NT) / fan2).astype(BF16)
    hidden_grad = matmul(down_two, second, NT)
    targets_grad = hidden_grad[:, :batch] + matmul(self2_ref[...], cot, NT)
    hidden_grad = jnp.concatenate([targets_grad, hidden_grad[:, batch:]], axis=1)
    pre_grad = (hidden_grad * (gate * (1.0 + preact * (1.0 - gate)))).astype(BF16)
    grads_ref[:width, :] = matmul(selfs, pre_grad, NT)
    grads_ref[width : 2 * width, :] = matmul(mean_one, pre_grad, NT)
    down_ref[...] = (matmul(agg1_ref[...], pre_grad) / fan1).astype(BF16)
    selfgrad_ref[...] = matmul(self1_ref[...], pre_grad)

    step_rows = 512
    for c in range(firsts // step_rows):
        at = c * step_rows
        spread_ref[:, at : at + step_rows] = (
            matmul(down_ref[...], table_ref[at : at + step_rows, :], NT)
            + selfgrad_ref[:, at : at + step_rows]
        ).astype(BF16)

    def spread(c, _):
        at = pl.multiple_of(c * step_rows, step_rows)
        spread_ref[:, pl.ds(at, step_rows)] = matmul(
            down_ref[...], table_ref[pl.ds(at, step_rows), :], NT
        ).astype(BF16)
        return 0

    lax.fori_loop(firsts // step_rows, inputs // step_rows, spread, 0, unroll=2)

    window = SPAN + 8
    merged_ref[...] = jnp.zeros(merged_ref.shape, F32)

    def merge(c, _):
        at = pl.multiple_of(c * SPAN, SPAN)
        low = jnp.minimum(ids_smem[0, at] // 8, (uniq - window) // 8) * 8
        low = pl.multiple_of(low, 8)
        place = lax.broadcasted_iota(jnp.int32, (window, SPAN), 0) + low
        picker = (ids_ref[:, pl.ds(at, SPAN)] == place).astype(F32).astype(BF16)
        merged_ref[pl.ds(low, window), :] += matmul(picker, spread_ref[:, pl.ds(at, SPAN)], NT)
        return 0

    lax.fori_loop(0, inputs // SPAN, merge, 0, unroll=4)
    picked_ref[...] = (merged_ref[...] * GRAD_SCALE).astype(BF16)

    group = GROUP
    chunk = group * tall
    quarter = width // REPS
    label_line = (
        lax.broadcasted_iota(jnp.int32, (chunk, group), 0)
        == lax.broadcasted_iota(jnp.int32, (chunk, group), 1) * tall + half
    ).astype(F32).astype(BF16)

    def place_rows(c, _):
        at = pl.multiple_of(c * chunk, chunk)
        doms = pl.ds(pl.multiple_of(c * group, group), group)
        place = lax.broadcasted_iota(jnp.int32, (chunk, uniq), 0) + at
        first_half = matmul(
            (target_ref[0:1, :] == place).astype(F32).astype(BF16), picked_ref[...]
        )
        second_half = matmul(
            (target_ref[1:2, :] == place).astype(F32).astype(BF16), picked_ref[...]
        )
        labels = matmul(label_line, high_ref[doms, :].astype(BF16)) * 16.0 + matmul(
            label_line, low_ref[doms, :].astype(BF16)
        )
        for r in range(REPS):
            columns = slice(r * quarter, (r + 1) * quarter)
            line = jnp.concatenate([first_half[:, columns], second_half[:, columns]], axis=1)
            out_ref[pl.ds(pl.multiple_of(r * domains * tall + at, 8), chunk), :] = line + labels
        return 0

    lax.fori_loop(0, domains // group, place_rows, 0)


def add_kernel(capacity, lines_ref, table_ref):
    half = capacity // 2
    tall = half + 1
    sources = lines_ref.shape[0] // tall
    quarter = LANES // 2
    height = table_ref.shape[0]
    codes = lines_ref[pl.ds(half, sources, stride=tall), :]
    rows = codes.T.astype(jnp.int32) - 1
    blocks = jnp.right_shift(codes.astype(jnp.int32) - 1, height.bit_length() - 1)
    rows = jnp.where(rows < 0, -1, rows & (height - 1))
    left = lax.broadcasted_iota(jnp.int32, (sources, LANES), 1) < quarter
    sides = [jnp.where(left, 0, 1) + 2 * side for side in range(2)]
    place = lax.broadcasted_iota(jnp.int32, (height, sources), 0)
    table_ref[...] = jnp.zeros(table_ref.shape, F32)
    together = 5
    for start in range(0, half, together):
        pickers, wides = [], []
        for slot in range(start, min(start + together, half)):
            lines = lines_ref[pl.ds(slot, sources, stride=tall), :]
            swapped = pltpu.roll(lines, quarter, 1)
            for at, pair in (
                (slot, jnp.where(left, lines, swapped)),
                (slot + half, jnp.where(left, swapped, lines)),
            ):
                block = blocks[:, at : at + 1]
                kept = [jnp.where(block == side, pair, 0.0).astype(BF16) for side in sides]
                wides.append(jnp.concatenate(kept, axis=1))
                pickers.append((rows[at : at + 1, :] == place).astype(F32).astype(BF16))
        table_ref[...] += matmul(
            jnp.concatenate(pickers, axis=1), jnp.concatenate(wides, axis=0)
        )


def join_kernel(parts_ref, table_ref):
    height = parts_ref.shape[0] // REPS
    quarter = parts_ref.shape[1] // REPS
    for q in range(REPS):
        table_ref[q * height : (q + 1) * height, :] = jnp.concatenate(
            [
                parts_ref[r * height : (r + 1) * height, q * quarter : (q + 1) * quarter]
                for r in range(REPS)
            ],
            axis=1,
        )


VMEM = pl.BlockSpec(memory_space=pltpu.VMEM)
HBM = pl.BlockSpec(memory_space=pltpu.HBM)
PARAMS = pltpu.CompilerParams(vmem_limit_bytes=48 * 1024 * 1024)
LOCAL_PARAMS = pltpu.CompilerParams(vmem_limit_bytes=60 * 1024 * 1024)


def local_pass(capacity, domains, x, first, second, ids, owners, rows, cot, self1, agg1, self2, agg2):
    inputs, width = x.shape
    firsts = first.shape[1]
    uniq = owners.shape[1]
    arrays = (x, first, second, ids, owners, rows, cot, self1, agg1, self2, agg2)
    return pl.pallas_call(
        functools.partial(local_kernel, capacity),
        out_shape=(
            jax.ShapeDtypeStruct((REPS * domains * (capacity // 2 + 1), LANES), F32),
            jax.ShapeDtypeStruct((4 * width, width), F32),
        ),
        in_specs=[HBM] * 11,
        out_specs=(VMEM, VMEM),
        scratch_shapes=[
            pltpu.VMEM((width, inputs), BF16),
            pltpu.VMEM((inputs, firsts), BF16),
            pltpu.VMEM((width, firsts), BF16),
            pltpu.VMEM((width, firsts), BF16),
            pltpu.VMEM((width, firsts), F32),
            pltpu.VMEM((width, inputs), BF16),
            pltpu.VMEM((uniq, width), F32),
            pltpu.VMEM((uniq, width), BF16),
            pltpu.VMEM((2, uniq), jnp.int32),
            pltpu.VMEM((domains, LANES), F32),
            pltpu.VMEM((domains, LANES), F32),
            *[pltpu.VMEM(a.shape, a.dtype) for a in arrays],
            pltpu.SMEM(ids.shape, ids.dtype),
            pltpu.SemaphoreType.DMA((len(arrays) + 1,)),
        ],
        compiler_params=LOCAL_PARAMS,
        name="local_pass",
    )(*arrays)


def add_rows(capacity, lines):
    return pl.pallas_call(
        functools.partial(add_kernel, capacity),
        out_shape=jax.ShapeDtypeStruct((ROWS_OWN // REPS, 4 * (LANES // 2)), F32),
        in_specs=[VMEM],
        out_specs=VMEM,
        compiler_params=PARAMS,
        name="add_rows",
    )(lines)


def join_columns(parts):
    return pl.pallas_call(
        join_kernel,
        out_shape=jax.ShapeDtypeStruct(parts.shape, F32),
        in_specs=[VMEM],
        out_specs=VMEM,
        compiler_params=PARAMS,
        name="join_columns",
    )(parts)


def sum_over_domains(value, domains):
    place = lax.axis_index("dom")
    steps = [1 << bit for bit in range(domains.bit_length() - 1)]

    def swap(part, step):
        return lax.ppermute(part, "dom", [(i, i ^ step) for i in range(domains)])

    for step in steps:
        pairs = value.reshape(value.shape[0] // 2, 2, *value.shape[1:])
        upper = (place & step) != 0
        sent = jnp.where(upper, pairs[:, 0], pairs[:, 1])
        kept = jnp.where(upper, pairs[:, 1], pairs[:, 0])
        value = kept + swap(sent, step)
    return value[0]


def on_device(
    node_input,
    neighbor_first,
    neighbor_second,
    merge_ids,
    owner_ids,
    owner_rows,
    cotangent,
    self_first,
    agg_first,
    self_second,
    agg_second,
):
    target_total = cotangent.shape[0]
    width = node_input.shape[1]
    uniq_total = owner_rows.shape[0]
    domains = lax.axis_size("dom")
    factor = (domains * lax.axis_size("rep") * target_total) ** (-0.5)
    capacity = max(2, 5 * uniq_total // (4 * domains))
    outgoing, grads = local_pass(
        capacity,
        domains,
        node_input,
        neighbor_first.T,
        neighbor_second.T,
        merge_ids,
        owner_ids.T,
        owner_rows[None, :],
        cotangent,
        self_first,
        agg_first,
        self_second,
        agg_second,
    )
    arrived = lax.all_to_all(
        outgoing.reshape(REPS * domains, 1, -1), ("rep", "dom"), 0, 0, tiled=True
    )
    own_grads = lax.psum_scatter(grads, "rep", scatter_dimension=0, tiled=True)
    share = width // domains
    total = sum_over_domains(own_grads.reshape(domains, share, width), domains) * factor
    arrived, total = lax.optimization_barrier((arrived, total))
    place = lax.axis_index("rep")
    parts = [total] + [
        lax.ppermute(total, "rep", [(i, (i + step) % REPS) for i in range(REPS)])
        for step in range(1, REPS)
    ]
    totals = jnp.concatenate(
        [
            jnp.where(
                place == matrix,
                parts[0],
                jnp.where(
                    place == (matrix + 1) % REPS,
                    parts[1],
                    jnp.where(place == (matrix + 2) % REPS, parts[2], parts[3]),
                ),
            )
            for matrix in range(REPS)
        ],
        axis=0,
    )
    spread = lax.all_to_all(
        jnp.broadcast_to(totals[None], (domains, REPS * share, width)), "dom", 0, 0, tiled=True
    )
    weight_grads = (
        spread.reshape(domains, REPS, share, width)
        .transpose(1, 0, 2, 3)
        .reshape(REPS, width, width)
    )
    quarter = add_rows(capacity, arrived.reshape(-1, LANES))
    table = join_columns(lax.all_gather(quarter, "rep", axis=0, tiled=True))
    return (table, weight_grads)


def solution(mesh):
    placed = (
        P(("dom", "rep"), None),
        P(("dom", "rep"), None),
        P(("dom", "rep"), None),
        P(("dom", "rep"), None),
        P(("dom", "rep"), None),
        P(("dom", "rep")),
        P(("dom", "rep"), None),
        P(),
        P(),
        P(),
        P(),
    )
    return jax.shard_map(
        on_device, mesh=mesh, in_specs=placed, out_specs=(P("dom", None), P()), check_vma=False
    )
```
